512 devices in a mesh: vol: 32 (over z, core), view: 16 (over y, x).
Axes of the slice: x: 4, y: 4, z: 16, core: 2. Of those that a mesh axis runs over, the one named last changes fastest.
Arguments:
- volume: float32 [256, 1024], P('vol'), may hold values from -240 to 240
- footprint: int32 [32, 16, 32], P(None, 'view'), may hold values from 0 to 255, as said below
- offsets: int32 [32, 16, 32], P('vol', 'view'), may hold values from 0 to 1023
- ray_weights: bfloat16 [32, 16, 32, 4, 8192], P('vol', 'view'), may hold values from 0.049804688 to 1
- measured: float32 [32, 16, 8192], P('vol', 'view'), may hold values from -240 to 240
Outputs:
- correction: float32 [256, 1024], P('vol', 'view')
The draws below stay inside these ranges and needn't reach their ends.
Inputs may be any that keep to these rules, and one draw needn't show every extreme that they name: Block b is owned by index b // 8 of vol. Each list footprint[o, g] names 32 distinct blocks: for some r and c, the blocks (r + i) * 8 + c + j for i < 16 and j < 2, in that order (i major).
All inputs are finite; a program needn't handle non-finite values.
Results may differ from the reference program's by a relative error of at most 0.0003.
Values sent between devices are 32-bit elements; how exact they have to be, the bound alone decides.
No kernel may reach another device: no remote copies, remote signals or barrier semaphores. Data moves between devices by JAX's collectives and lax.ppermute only.
A program may use at most 64 MiB of HBM per device.

```python
import math
import jax
import jax.numpy as jnp
from jax import lax

DET = 8192
VOXELS = 1024
BLK_DEV = 8
BLOCKS = 256
FOOT_ROWS = 16
FOOT_COLS = 2
FOOT = 32
BAND = 4
N_VOL = 32
N_VIEW = 16


def draw_footprint(key, part):
    key = jax.random.fold_in(key, 7)
    key_rows, key_cols = jax.random.split(key)
    row_start = jax.random.randint(key_rows, (N_VOL, N_VIEW), 0, N_VOL - FOOT_ROWS + 1)
    col_start = jax.random.randint(key_cols, (N_VOL, N_VIEW), 0, BLK_DEV - FOOT_COLS + 1)
    row_start = row_start.at[0, 0].set(0).at[N_VOL - 1, N_VIEW - 1].set(N_VOL - FOOT_ROWS)
    col_start = col_start.at[0, 0].set(0).at[N_VOL - 1, N_VIEW - 1].set(BLK_DEV - FOOT_COLS)
    row_index = jnp.arange(FOOT_ROWS)[:, None]
    col_index = jnp.arange(FOOT_COLS)[None, :]
    covered = (row_start[:, :, None, None] + row_index) * BLK_DEV + col_start[:, :, None, None] + col_index
    return covered.reshape(N_VOL, N_VIEW, FOOT).astype(jnp.int32)


def touch_ends(array, key, low, top_value):
    dims = array.shape
    index_at = [jax.random.randint(jax.random.fold_in(key, axis), (), 0, dims[axis]) for axis in range(len(dims))]
    array = array.at[tuple(index_at)].set(low)
    longest = dims.index(max(dims))
    index_at[longest] = (index_at[longest] + 1) % dims[longest]
    return array.at[tuple(index_at)].set(top_value)


def steps_of(own_key, extent, cuts, smallest, largest):
    def one(axis_at, blocks):
        heights = jax.random.uniform(jax.random.fold_in(jax.random.fold_in(own_key, 6), axis_at), (blocks,), jnp.float32, smallest / len(cuts), largest / len(cuts))
        return jnp.repeat(jnp.exp(heights), extent[axis_at] // blocks).reshape((-1,) + (1,) * (len(extent) - axis_at - 1))

    factor_of = one(*cuts[0])
    for cut in cuts[1:]:
        factor_of = factor_of * one(*cut)
    return factor_of


def normal_values(key, extent, deviation, reach, cuts=(), kind=jnp.bfloat16):
    gain = steps_of(key, extent, cuts, -0.22, 0.18) if cuts else 1.0
    values = jax.random.normal(key, extent, jnp.float32) * deviation * gain
    return jnp.minimum(jnp.maximum(values, -reach), reach).astype(kind)


def setup_inputs(seed: int = 0) -> dict:
    streams_of = jax.random.split(jax.random.key(seed), 6)
    return {
        "volume": normal_values(streams_of[0], (BLOCKS, VOXELS), 30.0, 240.0, ((0, 32),), jnp.float32),
        "footprint": draw_footprint(jax.random.fold_in(streams_of[5], 71), 0),
        "offsets": touch_ends(jax.random.randint(streams_of[2], (N_VOL, N_VIEW, FOOT), 0, VOXELS), jax.random.fold_in(streams_of[2], 1), 0, VOXELS - 1).astype(jnp.int32),
        "ray_weights": jnp.clip(jnp.exp(math.log(1.0) - 2.9996462 * jax.random.uniform(streams_of[3], (N_VOL, N_VIEW, FOOT, BAND, DET), jnp.float32) ** steps_of(streams_of[3], (N_VOL, N_VIEW, FOOT, BAND, DET), ((0, 32), (1, 16)), -0.2, 0.2)), 0.049804688, 1.0).astype(jnp.bfloat16),
        "measured": normal_values(streams_of[4], (N_VOL, N_VIEW, DET), 30.0, 240.0, ((0, 32), (1, 16)), jnp.float32),
    }


def project(blocks, starts, ray_weights):
    band_len = ray_weights.shape[1]
    det_len = ray_weights.shape[2]
    voxels = blocks.shape[1]
    copies = (det_len + band_len) // voxels + 2
    repeated = jnp.tile(blocks, (1, copies))
    windows = jax.vmap(lambda one_row, first: lax.dynamic_slice_in_dim(one_row, first, det_len + band_len))(repeated, starts)
    stacked = jnp.stack([windows[:, lag_index:lag_index + det_len] for lag_index in range(band_len)], axis=1)
    return lax.optimization_barrier(jnp.sum(ray_weights * stacked, axis=(0, 1)))

def backproject(blocks, starts, ray_weights, residual_rays):
    _, pullback = jax.vjp(lambda volume_part: project(volume_part, starts, ray_weights), blocks)
    cotangents = jnp.stack([residual_rays, jnp.ones_like(residual_rays)])
    pulled = jax.vmap(lambda cotangent: pullback(cotangent)[0])(cotangents)
    return jnp.transpose(pulled, (1, 0, 2))

def reference(volume, footprint, offsets, ray_weights, measured):
    block_lists = footprint.reshape(-1, FOOT)
    start_lists = offsets.reshape(-1, FOOT)
    weight_sets = ray_weights.reshape(-1, FOOT, BAND, DET)
    measured_sets = measured.reshape(-1, DET)

    def add_device(accumulated, inputs):
        covered, starts, weight_set, measured_set = inputs
        blocks = jnp.take(volume, covered, axis=0)
        projection = project(blocks, starts, weight_set)
        row_sum = lax.optimization_barrier(jnp.sum(weight_set, axis=(0, 1), dtype=jnp.float32))
        residual_rays = (measured_set - projection) / row_sum
        partials = backproject(blocks, starts, weight_set, residual_rays)
        return (accumulated.at[covered].add(partials), None)
    initial = jnp.zeros((BLOCKS, 2, VOXELS), jnp.float32)
    accumulated, _ = lax.scan(add_device, initial, (block_lists, start_lists, weight_sets, measured_sets))
    return accumulated[:, 0] / jnp.maximum(accumulated[:, 1], 1.0)
```

```python
import functools

import jax
import jax.numpy as jnp
from jax import lax
from jax.experimental import pallas as pl
from jax.experimental.pallas import tpu as pltpu
from jax.sharding import PartitionSpec as P

VOXELS = 1024
LANES = 128
TILES = VOXELS // LANES
FOOT = 32
BAND = 4
FOLDS = 8
BLK = 8
N_Z = 16
N_VIEW = 16
MSG = FOOT + 8
SUB = VOXELS // N_VIEW

VMEM = pl.BlockSpec(memory_space=pltpu.VMEM)
SMEM = pl.BlockSpec(memory_space=pltpu.SMEM)
F32 = jnp.float32
BF16 = jnp.bfloat16


def rotate_left(rows, amount):
    amount %= VOXELS
    return rows if amount == 0 else pltpu.roll(rows, VOXELS - amount, 1)


def rotate_right(rows, amount):
    return rotate_left(rows, VOXELS - amount)


def rotate_each(rows, counts, rotate):
    wide = jnp.concatenate([counts] * TILES, axis=1)
    for bit in range(10):
        rows = jnp.where((wide >> bit) & 1 == 1, rotate(rows, 1 << bit), rows)
    return rows


def split3(x):
    high = x.astype(BF16)
    rest = x - high.astype(F32)
    mid = rest.astype(BF16)
    low = (rest - mid.astype(F32)).astype(BF16)
    return high, mid, low


def fold_lags(spread_ref, counts):
    total = spread_ref[BAND - 1]
    for lag in range(BAND - 2, -1, -1):
        total = rotate_right(total, 1) + spread_ref[lag]
    return rotate_each(total, counts, rotate_right)


def weight_tile(weights_ref, lag, fold, tile):
    first = pl.multiple_of(fold * VOXELS + tile * LANES, LANES)
    return weights_ref[lag, :, pl.ds(first, LANES)].astype(F32)


def sum_rows(tile):
    part = tile[0:8] + tile[8:16] + tile[16:24] + tile[24:32]
    return jnp.sum(part, axis=0, keepdims=True)


def pick_kernel(core_ref, foot_ref, own_ref, other_ref, out_ref, rows_ref):
    core = core_ref[0]
    for side, ref in enumerate((own_ref, other_ref)):
        for tile in range(TILES):
            rows_ref[pl.ds(side * BLK * TILES + tile, BLK, stride=TILES), :] = ref[:, tile * LANES : (tile + 1) * LANES]
    for z in range(N_Z):
        column = foot_ref[2 * z + core, 0] & (BLK - 1)
        for side in range(2):
            first = pl.multiple_of((side * BLK + column) * TILES, TILES)
            out_ref[z, side * 2 * TILES : (side + 1) * 2 * TILES, :] = rows_ref[pl.ds(first, 2 * TILES), :]


def sums_kernel(weights_ref, counts_ref, column_ref, row_ref, spread_ref):
    def tile_step(tile, carry):
        lanes = pl.ds(pl.multiple_of(tile * LANES, LANES), LANES)
        spread = [jnp.zeros((FOOT, LANES), F32) for _ in range(BAND)]
        rows = []
        for fold in range(FOLDS):
            total = jnp.zeros((FOOT, LANES), F32)
            for lag in range(BAND):
                weights = weight_tile(weights_ref, lag, fold, tile)
                spread[lag] = spread[lag] + weights
                total = total + weights
            rows.append(sum_rows(total))
        row_ref[:, lanes] = jnp.concatenate(rows, axis=0)
        for lag in range(BAND):
            spread_ref[lag, :, lanes] = spread[lag]
        return carry

    lax.fori_loop(0, TILES, tile_step, 0)
    column_ref[...] = fold_lags(spread_ref, counts_ref[...])


def rays_kernel(
    place_ref, blocks_ref, weights_ref, counts_ref, measured_ref, row_ref, column_ref, out_ref, window_ref, spread_ref
):
    core, first_block = place_ref[0], place_ref[1]
    first_owner = first_block >> 3
    shape = (FOOT, 2 * FOOT)
    foot = lax.broadcasted_iota(jnp.int32, shape, 0)
    slot = lax.broadcasted_iota(jnp.int32, shape, 1)
    owner = first_owner + (foot >> 1)
    side = (owner & 1) ^ core
    wanted = (side * 2 + (foot & 1)) * N_Z + (owner >> 1)
    chosen = (slot == wanted).astype(F32).astype(BF16)
    chosen = jnp.concatenate([chosen] * 3, axis=1)
    pieces = []
    for tile in range(TILES):
        rows = [blocks_ref[pl.ds(line * TILES + tile, N_Z, stride=4 * TILES), :] for line in range(4)]
        pieces.append(jnp.concatenate(rows, axis=0))
    sent = jnp.concatenate(pieces, axis=1)
    covered = jnp.dot(chosen, jnp.concatenate(split3(sent), axis=0), preferred_element_type=F32)
    counts = counts_ref[...]
    window = rotate_each(covered, counts, rotate_left)
    window_ref[0] = window
    for lag in range(1, BAND):
        window_ref[lag] = rotate_left(window, lag)

    def tile_step(tile, carry):
        lanes = pl.ds(pl.multiple_of(tile * LANES, LANES), LANES)
        rows = []
        windows = [window_ref[lag, :, lanes] for lag in range(BAND)]
        for fold in range(FOLDS):
            total = weight_tile(weights_ref, 0, fold, tile) * windows[0]
            for lag in range(1, BAND):
                total = total + weight_tile(weights_ref, lag, fold, tile) * windows[lag]
            rows.append(sum_rows(total))
        projection = jnp.concatenate(rows, axis=0)
        residual = (measured_ref[:, lanes] - projection) / row_ref[:, lanes]
        for lag in range(BAND):
            spread = weight_tile(weights_ref, lag, 0, tile) * residual[0:1]
            for fold in range(1, FOLDS):
                spread = spread + weight_tile(weights_ref, lag, fold, tile) * residual[fold : fold + 1]
            spread_ref[lag, :, lanes] = spread
        return carry

    lax.fori_loop(0, TILES, tile_step, 0)
    back = fold_lags(spread_ref, counts)
    low = lax.broadcasted_iota(jnp.int32, (FOOT, LANES), 1) < SUB
    base = jnp.full((8, LANES), first_block, jnp.int32).astype(F32)
    for tile in range(TILES):
        sums = back[:, tile * LANES : (tile + 1) * LANES]
        columns = column_ref[:, tile * LANES : (tile + 1) * LANES]
        out_ref[2 * tile, 0:FOOT, :] = jnp.where(low, sums, pltpu.roll(columns, SUB, 1))
        out_ref[2 * tile + 1, 0:FOOT, :] = jnp.where(low, pltpu.roll(sums, SUB, 1), columns)
        out_ref[2 * tile, FOOT:MSG, :] = base
        out_ref[2 * tile + 1, FOOT:MSG, :] = base


def place_kernel(parts_ref, out_ref):
    lane = lax.broadcasted_iota(jnp.int32, (1, LANES), 1)
    within = (((lane & (FOOT - 1)) >> 1) * BLK + (lane & 1)).astype(F32)
    quarter = lane >> 5
    targets = []
    for group in range(0, N_VIEW, 4):
        first = parts_ref[group, FOOT : FOOT + 1, :]
        for other in range(1, 4):
            first = jnp.where(quarter == other, parts_ref[group + other, FOOT : FOOT + 1, :], first)
        targets.append(first + within)
    target = jnp.concatenate(targets, axis=1)
    block = lax.broadcasted_iota(jnp.int32, (2 * FOLDS * N_Z, N_VIEW * FOOT), 0).astype(F32)
    chosen = jnp.where(block == target, 1.0, 0.0).astype(BF16)
    parts = jnp.concatenate([parts_ref[group, 0:FOOT, :] for group in range(N_VIEW)], axis=0)
    high, mid, low = split3(parts)
    both = jnp.dot(chosen, jnp.concatenate([high, mid], axis=1), preferred_element_type=F32)
    total = both[:, :LANES] + (both[:, LANES:] + jnp.dot(chosen, low, preferred_element_type=F32))
    out_ref[...] = total


def finish_kernel(mine_ref, theirs_ref, out_ref):
    total = mine_ref[...] + theirs_ref[...]
    columns = pltpu.roll(total, SUB, 1)
    out_ref[...] = (total / jnp.maximum(columns, 1.0))[:, :SUB]


def call(kernel, out_shape, in_specs, scratch=(), cost=None):
    return pl.pallas_call(
        kernel,
        out_shape=out_shape,
        in_specs=in_specs,
        out_specs=jax.tree.map(lambda _: VMEM, out_shape),
        scratch_shapes=scratch,
        cost_estimate=cost,
        compiler_params=pltpu.CompilerParams(vmem_limit_bytes=24 * 2**20),
    )


def shards(volume, footprint, offsets, ray_weights, measured):
    member = lax.axis_index("vol")
    core = member & 1
    swap = [(i, i ^ 1) for i in range(2 * N_Z)]
    chips = [[2 * z + c for z in range(N_Z)] for c in range(2)]
    lists = footprint[:, 0, :]

    other = lax.ppermute(volume, "vol", swap)
    sent = call(
        pick_kernel,
        jax.ShapeDtypeStruct((N_Z, 4 * TILES, LANES), F32),
        [SMEM, SMEM, VMEM, VMEM],
        [pltpu.VMEM((2 * BLK * TILES, LANES), F32)],
    )(core[None], lists, volume, other)
    blocks = lax.all_to_all(sent, "vol", 0, 0, axis_index_groups=chips)

    weights = jnp.transpose(ray_weights[0, 0], (1, 0, 2))
    counts = jnp.broadcast_to(offsets[0, 0][:, None], (FOOT, LANES))
    work = BAND * FOOT * FOLDS * VOXELS
    columns, row_sum = call(
        sums_kernel,
        (jax.ShapeDtypeStruct((FOOT, VOXELS), F32), jax.ShapeDtypeStruct((FOLDS, VOXELS), F32)),
        [VMEM, VMEM],
        [pltpu.VMEM((BAND, FOOT, VOXELS), F32)],
        pl.CostEstimate(flops=2 * work, bytes_accessed=2 * work, transcendentals=0),
    )(weights, counts)

    first_block = lax.dynamic_index_in_dim(lists, member, 0, keepdims=False)[0]
    parts = call(
        rays_kernel,
        jax.ShapeDtypeStruct((N_VIEW, MSG, LANES), F32),
        [SMEM] + [VMEM] * 6,
        [pltpu.VMEM((BAND, FOOT, VOXELS), F32), pltpu.VMEM((BAND, FOOT, VOXELS), F32)],
        pl.CostEstimate(flops=4 * work, bytes_accessed=2 * work, transcendentals=0),
    )(
        jnp.stack([core, first_block]),
        blocks.reshape(N_Z * 4 * TILES, LANES),
        weights,
        counts,
        measured.reshape(FOLDS, VOXELS),
        row_sum,
        columns,
    )
    parts = lax.all_to_all(parts, "view", 0, 0)
    placed = call(place_kernel, jax.ShapeDtypeStruct((N_Z * 2 * BLK, LANES), F32), [VMEM])(parts)
    placed = lax.all_to_all(placed.reshape(N_Z, 2, BLK, LANES), "vol", 0, 0, axis_index_groups=chips)
    summed = jnp.sum(placed, axis=0)
    mine = lax.dynamic_index_in_dim(summed, core, 0, keepdims=False)
    theirs = lax.ppermute(lax.dynamic_index_in_dim(summed, 1 - core, 0, keepdims=False), "vol", swap)
    return call(finish_kernel, jax.ShapeDtypeStruct((BLK, SUB), F32), [VMEM, VMEM])(mine, theirs)


def solution(mesh):
    in_specs = (
        P("vol", None),
        P(None, "view", None),
        P("vol", "view", None),
        P("vol", "view", None, None, None),
        P("vol", "view", None),
    )
    return jax.shard_map(shards, mesh=mesh, in_specs=in_specs, out_specs=P("vol", "view"), check_vma=False)
```

```python
import jax
import jax.numpy as jnp
from jax import lax
from jax.experimental import pallas as pl
from jax.experimental.pallas import tpu as pltpu
from jax.sharding import PartitionSpec as P

VOXELS = 1024
LANES = 128
TILES = VOXELS // LANES
FOOT = 32
HALF = FOOT // 2
BAND = 4
FOLDS = 8
BLK = 8
N_Z = 16
N_VIEW = 16
PEERS = 2 * N_VIEW
MSG = HALF + 8
SUB = VOXELS // N_VIEW

VMEM = pl.BlockSpec(memory_space=pltpu.VMEM)
SMEM = pl.BlockSpec(memory_space=pltpu.SMEM)
ANY = pl.BlockSpec(memory_space=pl.ANY)
F32 = jnp.float32
BF16 = jnp.bfloat16


def lane_tiles(rows):
    return [rows[:, tile * LANES : (tile + 1) * LANES] for tile in range(TILES)]


def rotate_each(tiles, counts, left):
    lane = lax.broadcasted_iota(jnp.int32, (FOOT, LANES), 1)
    within = counts & (LANES - 1)
    source = (lane + within if left else lane - within) & (LANES - 1)
    same = lane + within < LANES if left else lane >= within
    step = 1 if left else TILES - 1
    moved = [jnp.take_along_axis(tile, source, axis=1) for tile in tiles]
    tiles = [jnp.where(same, moved[t], moved[(t + step) % TILES]) for t in range(TILES)]
    for bit in range(3):
        far = step << bit
        chosen = (counts >> (7 + bit)) & 1 == 1
        tiles = [jnp.where(chosen, tiles[(t + far) % TILES], tiles[t]) for t in range(TILES)]
    return tiles


def split3(x):
    high = x.astype(BF16)
    rest = x - high.astype(F32)
    mid = rest.astype(BF16)
    low = (rest - mid.astype(F32)).astype(BF16)
    return high, mid, low


def fold_lags(spread_ref, counts):
    total = spread_ref[BAND - 1]
    for lag in range(BAND - 2, -1, -1):
        total = pltpu.roll(total, 1, 1) + spread_ref[lag]
    return rotate_each(lane_tiles(total), counts, False)


def sum_rows(totals):
    row = lax.broadcasted_iota(jnp.int32, (8, LANES), 0)
    low = row < 4
    fours = [
        jnp.where(low, totals[k], totals[k + 4]) + pltpu.roll(jnp.where(low, totals[k + 4], totals[k]), 4, 0)
        for k in range(4)
    ]

    def halve(parts, width):
        first = row & width == 0
        count = len(parts) // 2
        return [
            jnp.where(
                first,
                parts[k] + pltpu.roll(parts[k], 8 - width, 0),
                parts[k + count] + pltpu.roll(parts[k + count], width, 0),
            )
            for k in range(count)
        ]

    return halve(halve(fours, 2), 1)[0]


def quarter(tile):
    return tile[0:8] + tile[8:16] + tile[16:24] + tile[24:32]


def lanes_of(fold, tile):
    return pl.ds(pl.multiple_of(fold * VOXELS + tile * LANES, LANES), LANES)


def pick_kernel(core_ref, foot_hbm, own_hbm, other_ref, out_ref, rows_ref, own_ref, foot_ref, sems):
    foot_copy = pltpu.make_async_copy(foot_hbm, foot_ref, sems.at[0])
    own_copy = pltpu.make_async_copy(own_hbm, own_ref, sems.at[1])
    foot_copy.start()
    own_copy.start()
    core = core_ref[0]

    def spread_rows(side, ref):
        for tile in range(TILES):
            rows_ref[pl.ds(side * BLK * TILES + tile, BLK, stride=TILES), :] = ref[:, tile * LANES : (tile + 1) * LANES]

    spread_rows(1, other_ref)
    own_copy.wait()
    spread_rows(0, own_ref)
    foot_copy.wait()
    for z in range(N_Z):
        column = foot_ref[2 * z + core, 0, 0] & (BLK - 1)
        for side in range(2):
            first = pl.multiple_of((side * BLK + column) * TILES, TILES)
            out_ref[z, side * 2 * TILES : (side + 1) * 2 * TILES, :] = rows_ref[pl.ds(first, 2 * TILES), :]


def sums_kernel(weights_ref, counts_ref, wide_ref, column_ref, turned_ref, row_ref, spread_ref):
    def tile_step(tile, carry):
        spread = [jnp.zeros((FOOT, LANES), F32) for _ in range(BAND)]
        rows = []
        for fold in range(FOLDS):
            total = jnp.zeros((FOOT, LANES), F32)
            for lag in range(BAND):
                weights = weights_ref[lag, :, lanes_of(fold, tile)].astype(F32)
                wide_ref[lag, :, lanes_of(fold, tile)] = weights
                spread[lag] = spread[lag] + weights
                total = total + weights
            rows.append(quarter(total))
        row_ref[:, lanes_of(0, tile)] = sum_rows(rows)
        for lag in range(BAND):
            spread_ref[lag, :, lanes_of(0, tile)] = spread[lag]
        return carry

    lax.fori_loop(0, TILES, tile_step, 0)
    for tile, columns in enumerate(fold_lags(spread_ref, counts_ref[...])):
        column_ref[:, tile * LANES : (tile + 1) * LANES] = columns
        turned_ref[:, tile * LANES : (tile + 1) * LANES] = pltpu.roll(columns, SUB, 1)


def rays_kernel(
    place_ref,
    blocks_ref,
    wide_ref,
    counts_ref,
    measured_ref,
    row_ref,
    column_ref,
    turned_ref,
    out_ref,
    window_ref,
    spread_ref,
):
    core, first_block = place_ref[0], place_ref[1]
    first_owner = first_block >> 3
    odd = first_owner & 1
    double = 2 * lax.broadcasted_iota(jnp.int32, (8, LANES), 0)
    covered = [[] for _ in range(TILES)]
    for step in range(2):
        parity = step ^ odd
        side = parity ^ core
        near = double + parity >= first_owner
        turn = (8 - (((first_owner + 1 - parity) >> 1) & 7)) & 7
        for column in range(2):
            for tile in range(TILES):
                rows = blocks_ref[pl.ds((side * 2 + column) * TILES + tile, N_Z, stride=4 * TILES), :]
                covered[tile].append(pltpu.roll(jnp.where(near, rows[0:8], rows[8:16]), turn, 0))
    counts = counts_ref[...]
    window = jnp.concatenate(rotate_each([jnp.concatenate(c, axis=0) for c in covered], counts, True), axis=1)
    window_ref[0] = window
    for lag in range(1, BAND):
        window_ref[lag] = pltpu.roll(window, VOXELS - lag, 1)

    def tile_step(tile, carry):
        lanes = lanes_of(0, tile)
        windows = [window_ref[lag, :, lanes] for lag in range(BAND)]
        rows = []
        for fold in range(FOLDS):
            total = wide_ref[0, :, lanes_of(fold, tile)] * windows[0]
            for lag in range(1, BAND):
                total = total + wide_ref[lag, :, lanes_of(fold, tile)] * windows[lag]
            rows.append(quarter(total))
        residual = (measured_ref[:, lanes] - sum_rows(rows)) / row_ref[:, lanes]
        shares = [residual[fold : fold + 1] for fold in range(FOLDS)]
        for lag in range(BAND):
            spread = wide_ref[lag, :, lanes] * shares[0]
            for fold in range(1, FOLDS):
                spread = spread + wide_ref[lag, :, lanes_of(fold, tile)] * shares[fold]
            spread_ref[lag, :, lanes] = spread
        return carry

    lax.fori_loop(0, TILES, tile_step, 0)
    low = lax.broadcasted_iota(jnp.int32, (HALF, LANES), 1) < SUB
    back = fold_lags(spread_ref, counts)
    for step in range(2):
        parity = step ^ odd
        first = parity * N_VIEW
        base = (((first_owner + 1 - parity) >> 1) << 3) + (first_block & 7)
        base = jnp.full((8, LANES), base, jnp.int32).astype(F32)
        part = slice(step * HALF, (step + 1) * HALF)
        for tile in range(TILES):
            lanes = slice(tile * LANES, (tile + 1) * LANES)
            sums = back[tile][part]
            out_ref[first + 2 * tile, 0:HALF, :] = jnp.where(low, sums, turned_ref[part, lanes])
            out_ref[first + 2 * tile + 1, 0:HALF, :] = jnp.where(low, pltpu.roll(sums, SUB, 1), column_ref[part, lanes])
            out_ref[first + 2 * tile, HALF:MSG, :] = base
            out_ref[first + 2 * tile + 1, HALF:MSG, :] = base


def place_kernel(parts_ref, out_ref):
    lane = lax.broadcasted_iota(jnp.int32, (1, LANES), 1)
    within = ((lane & 7) * BLK + ((lane >> 3) & 1)).astype(F32)
    source = lane >> 4
    targets = []
    for group in range(0, PEERS, 8):
        first = parts_ref[group, HALF : HALF + 1, :]
        for other in range(1, 8):
            first = jnp.where(source == other, parts_ref[group + other, HALF : HALF + 1, :], first)
        targets.append(first + within)
    target = jnp.concatenate(targets, axis=1)
    block = lax.broadcasted_iota(jnp.int32, (N_Z * BLK, PEERS * HALF), 0).astype(F32)
    chosen = jnp.where(block == target, 1.0, 0.0).astype(BF16)
    parts = jnp.concatenate([parts_ref[peer, 0:HALF, :] for peer in range(PEERS)], axis=0)
    high, mid, low = split3(parts)
    both = jnp.dot(chosen, jnp.concatenate([high, mid], axis=1), preferred_element_type=F32)
    total = both[:, :LANES] + (both[:, LANES:] + jnp.dot(chosen, low, preferred_element_type=F32))
    out_ref[...] = total


def finish_kernel(parts_ref, out_ref):
    total = parts_ref[0]
    for z in range(1, N_Z):
        total = total + parts_ref[z]
    columns = pltpu.roll(total, SUB, 1)
    out_ref[...] = (total / jnp.maximum(columns, 1.0))[:, :SUB]


def call(kernel, out_shape, in_specs, scratch=(), cost=None, limit=32):
    return pl.pallas_call(
        kernel,
        out_shape=out_shape,
        in_specs=in_specs,
        out_specs=jax.tree.map(lambda _: VMEM, out_shape),
        scratch_shapes=scratch,
        cost_estimate=cost,
        compiler_params=pltpu.CompilerParams(vmem_limit_bytes=limit * 2**20),
    )


def shards(volume, footprint, offsets, ray_weights, measured):
    member = lax.axis_index("vol")
    core = member & 1
    swap = [(i, i ^ 1) for i in range(2 * N_Z)]
    chips = [[2 * z + c for z in range(N_Z)] for c in range(2)]
    planes = [[z * PEERS + peer for peer in range(PEERS)] for z in range(N_Z)]

    other = lax.ppermute(volume, "vol", swap)
    sent = call(
        pick_kernel,
        jax.ShapeDtypeStruct((N_Z, 4 * TILES, LANES), F32),
        [SMEM, ANY, ANY, VMEM],
        [
            pltpu.VMEM((2 * BLK * TILES, LANES), F32),
            pltpu.VMEM((BLK, VOXELS), F32),
            pltpu.SMEM((2 * N_Z, 1, FOOT), jnp.int32),
            pltpu.SemaphoreType.DMA((2,)),
        ],
    )(core[None], footprint, volume, other)
    blocks = lax.all_to_all(sent, "vol", 0, 0, axis_index_groups=chips)

    weights = ray_weights.reshape(8, 2, 2, BAND, FOLDS * VOXELS)
    weights = jnp.transpose(weights, (3, 1, 2, 0, 4)).reshape(BAND, FOOT, FOLDS * VOXELS)
    counts = jnp.transpose(offsets.reshape(8, 2, 2), (1, 2, 0)).reshape(FOOT, 1)
    counts = jnp.broadcast_to(counts, (FOOT, LANES))
    work = BAND * FOOT * FOLDS * VOXELS
    wide, columns, turned, row_sum = call(
        sums_kernel,
        (
            jax.ShapeDtypeStruct((BAND, FOOT, FOLDS * VOXELS), F32),
            jax.ShapeDtypeStruct((FOOT, VOXELS), F32),
            jax.ShapeDtypeStruct((FOOT, VOXELS), F32),
            jax.ShapeDtypeStruct((FOLDS, VOXELS), F32),
        ),
        [VMEM, VMEM],
        [pltpu.VMEM((BAND, FOOT, VOXELS), F32)],
        pl.CostEstimate(flops=2 * work, bytes_accessed=6 * work, transcendentals=0),
    )(weights, counts)

    first_block = lax.dynamic_index_in_dim(footprint[:, 0, 0], member, 0, keepdims=False)
    parts = call(
        rays_kernel,
        jax.ShapeDtypeStruct((PEERS, MSG, LANES), F32),
        [SMEM] + [VMEM] * 7,
        [pltpu.VMEM((BAND, FOOT, VOXELS), F32), pltpu.VMEM((BAND, FOOT, VOXELS), F32)],
        pl.CostEstimate(flops=4 * work, bytes_accessed=4 * work, transcendentals=0),
    )(
        jnp.stack([core, first_block]),
        blocks.reshape(N_Z * 4 * TILES, LANES),
        wide,
        counts,
        measured.reshape(FOLDS, VOXELS),
        row_sum,
        columns,
        turned,
    )
    parts = lax.all_to_all(parts, ("vol", "view"), 0, 0, axis_index_groups=planes)
    placed = call(place_kernel, jax.ShapeDtypeStruct((N_Z * BLK, LANES), F32), [VMEM])(parts)
    placed = lax.all_to_all(placed.reshape(N_Z, BLK, LANES), "vol", 0, 0, axis_index_groups=chips)
    return call(finish_kernel, jax.ShapeDtypeStruct((BLK, SUB), F32), [VMEM])(placed)


def solution(mesh):
    in_specs = (
        P("vol", None),
        P(None, "view", None),
        P("vol", "view", None),
        P("vol", "view", None, None, None),
        P("vol", "view", None),
    )
    return jax.shard_map(shards, mesh=mesh, in_specs=in_specs, out_specs=P("vol", "view"), check_vma=False)
```

```python
import jax
import jax.numpy as jnp
from jax import lax
from jax.experimental import pallas as pl
from jax.experimental.pallas import tpu as pltpu
from jax.sharding import PartitionSpec as P

VOXELS = 1024
LANES = 128
TILES = VOXELS // LANES
FOOT = 32
HALF = FOOT // 2
BAND = 4
FOLDS = 8
BLK = 8
N_Z = 16
N_VIEW = 16
PEERS = 2 * N_VIEW
MSG = HALF + 8
SUB = VOXELS // N_VIEW
FIRST_Z = 8
FIRST_VIEW = 10

VMEM = pl.BlockSpec(memory_space=pltpu.VMEM)
SMEM = pl.BlockSpec(memory_space=pltpu.SMEM)
HBM = pl.BlockSpec(memory_space=pltpu.HBM)
F32 = jnp.float32
BF16 = jnp.bfloat16


def lane_tiles(rows):
    return [rows[:, tile * LANES : (tile + 1) * LANES] for tile in range(TILES)]


def rotate_each(tiles, counts, left):
    lane = lax.broadcasted_iota(jnp.int32, (FOOT, LANES), 1)
    within = counts & (LANES - 1)
    source = (lane + within if left else lane - within) & (LANES - 1)
    same = lane + within < LANES if left else lane >= within
    step = 1 if left else TILES - 1
    moved = [jnp.take_along_axis(tile, source, axis=1) for tile in tiles]
    tiles = [jnp.where(same, moved[t], moved[(t + step) % TILES]) for t in range(TILES)]
    for bit in range(3):
        far = step << bit
        chosen = (counts >> (7 + bit)) & 1 == 1
        tiles = [jnp.where(chosen, tiles[(t + far) % TILES], tiles[t]) for t in range(TILES)]
    return tiles


def split3(x):
    high = x.astype(BF16)
    rest = x - high.astype(F32)
    mid = rest.astype(BF16)
    low = (rest - mid.astype(F32)).astype(BF16)
    return high, mid, low


def fold_lags(spread_ref, counts):
    total = spread_ref[BAND - 1]
    for lag in range(BAND - 2, -1, -1):
        total = pltpu.roll(total, 1, 1) + spread_ref[lag]
    return rotate_each(lane_tiles(total), counts, False)


def sum_rows(totals):
    row = lax.broadcasted_iota(jnp.int32, (8, LANES), 0)
    low = row < 4
    fours = [
        jnp.where(low, totals[k], totals[k + 4]) + pltpu.roll(jnp.where(low, totals[k + 4], totals[k]), 4, 0)
        for k in range(4)
    ]

    def halve(parts, width):
        first = row & width == 0
        count = len(parts) // 2
        return [
            jnp.where(
                first,
                parts[k] + pltpu.roll(parts[k], 8 - width, 0),
                parts[k + count] + pltpu.roll(parts[k + count], width, 0),
            )
            for k in range(count)
        ]

    return halve(halve(fours, 2), 1)[0]


def quarter(tile):
    return tile[0:8] + tile[8:16] + tile[16:24] + tile[24:32]


def lanes_of(fold, tile):
    if isinstance(tile, int):
        return slice(fold * VOXELS + tile * LANES, fold * VOXELS + (tile + 1) * LANES)
    return pl.ds(pl.multiple_of(fold * VOXELS + tile * LANES, LANES), LANES)


def pick_kernel(core_ref, foot_hbm, own_hbm, other_ref, out_ref, rows_ref, own_ref, foot_ref, sems):
    foot_copy = pltpu.make_async_copy(foot_hbm, foot_ref, sems.at[0])
    own_copy = pltpu.make_async_copy(own_hbm, own_ref, sems.at[1])
    foot_copy.start()
    own_copy.start()
    core = core_ref[0]

    def spread_rows(side, ref):
        for tile in range(TILES):
            rows_ref[pl.ds(side * BLK * TILES + tile, BLK, stride=TILES), :] = ref[:, tile * LANES : (tile + 1) * LANES]

    spread_rows(1, other_ref)
    own_copy.wait()
    spread_rows(0, own_ref)
    foot_copy.wait()
    for z in range(N_Z):
        column = foot_ref[2 * z + core, 0, 0] & (BLK - 1)
        for side in range(2):
            first = pl.multiple_of((side * BLK + column) * TILES, TILES)
            out_ref[z ^ FIRST_Z, side * 2 * TILES : (side + 1) * 2 * TILES, :] = rows_ref[pl.ds(first, 2 * TILES), :]


def sums_kernel(weights_ref, counts_ref, column_ref, turned_ref, row_ref, spread_ref):
    def tile_step(tile, carry):
        spread = [jnp.zeros((FOOT, LANES), F32) for _ in range(BAND)]
        rows = []
        for fold in range(FOLDS):
            total = jnp.zeros((FOOT, LANES), F32)
            for lag in range(BAND):
                weights = weights_ref[lag, :, lanes_of(fold, tile)].astype(F32)
                spread[lag] = spread[lag] + weights
                total = total + weights
            rows.append(quarter(total))
        row_ref[:, lanes_of(0, tile)] = sum_rows(rows)
        for lag in range(BAND):
            spread_ref[lag, :, lanes_of(0, tile)] = spread[lag]
        return carry

    lax.fori_loop(0, TILES, tile_step, 0)
    for tile, columns in enumerate(fold_lags(spread_ref, counts_ref[...])):
        column_ref[:, tile * LANES : (tile + 1) * LANES] = columns
        turned_ref[:, tile * LANES : (tile + 1) * LANES] = pltpu.roll(columns, SUB, 1)


def rays_kernel(
    place_ref,
    blocks_ref,
    weights_ref,
    counts_ref,
    measured_ref,
    row_ref,
    column_ref,
    turned_ref,
    out_ref,
    window_ref,
    spread_ref,
    share_ref,
):
    core, first_block = place_ref[0], place_ref[1]
    first_owner = first_block >> 3
    odd = first_owner & 1
    double = 2 * lax.broadcasted_iota(jnp.int32, (8, LANES), 0)
    covered = [[] for _ in range(TILES)]
    for step in range(2):
        parity = step ^ odd
        side = parity ^ core
        near = double + parity >= first_owner
        turn = (8 - (((first_owner + 1 - parity) >> 1) & 7)) & 7
        for column in range(2):
            for tile in range(TILES):
                rows = blocks_ref[pl.ds((side * 2 + column) * TILES + tile, N_Z, stride=4 * TILES), :]
                covered[tile].append(pltpu.roll(jnp.where(near, rows[8:16], rows[0:8]), turn, 0))
    counts = counts_ref[...]
    window = jnp.concatenate(rotate_each([jnp.concatenate(c, axis=0) for c in covered], counts, True), axis=1)
    window_ref[0] = window
    for lag in range(1, BAND):
        window_ref[lag] = pltpu.roll(window, VOXELS - lag, 1)

    for tile in range(TILES):
        lanes = lanes_of(0, tile)
        windows = [window_ref[lag, :, lanes] for lag in range(BAND)]
        rows = []
        for fold in range(FOLDS):
            total = weights_ref[0, :, lanes_of(fold, tile)].astype(F32) * windows[0]
            for lag in range(1, BAND):
                total = total + weights_ref[lag, :, lanes_of(fold, tile)].astype(F32) * windows[lag]
            rows.append(quarter(total))
        share_ref[:, lanes] = (measured_ref[:, lanes] - sum_rows(rows)) / row_ref[:, lanes]
    for tile in range(TILES):
        lanes = lanes_of(0, tile)
        for lag in range(BAND):
            spread = weights_ref[lag, :, lanes].astype(F32) * share_ref[0:1, lanes]
            for fold in range(1, FOLDS):
                spread = spread + weights_ref[lag, :, lanes_of(fold, tile)].astype(F32) * share_ref[fold : fold + 1, lanes]
            spread_ref[lag, :, lanes] = spread
    low = lax.broadcasted_iota(jnp.int32, (HALF, LANES), 1) < SUB
    back = fold_lags(spread_ref, counts)
    for step in range(2):
        parity = step ^ odd
        first = parity * N_VIEW
        even = [first + (2 * tile ^ FIRST_VIEW) for tile in range(TILES)]
        other = [first + (2 * tile + 1 ^ FIRST_VIEW) for tile in range(TILES)]
        base = (((first_owner + 1 - parity) >> 1) << 3) + (first_block & 7)
        base = jnp.full((8, LANES), base, jnp.int32).astype(F32)
        part = slice(step * HALF, (step + 1) * HALF)
        for tile in range(TILES):
            lanes = slice(tile * LANES, (tile + 1) * LANES)
            sums = back[tile][part]
            out_ref[even[tile], 0:HALF, :] = jnp.where(low, sums, turned_ref[part, lanes])
            out_ref[other[tile], 0:HALF, :] = jnp.where(low, pltpu.roll(sums, SUB, 1), column_ref[part, lanes])
            out_ref[even[tile], HALF:MSG, :] = base
            out_ref[other[tile], HALF:MSG, :] = base


def place_kernel(parts_ref, out_ref):
    lane = lax.broadcasted_iota(jnp.int32, (1, LANES), 1)
    within = ((lane & 7) * BLK + ((lane >> 3) & 1)).astype(F32)
    source = lane >> 4
    targets = []
    for group in range(0, PEERS, 8):
        first = parts_ref[group, HALF : HALF + 1, :]
        for other in range(1, 8):
            first = jnp.where(source == other, parts_ref[group + other, HALF : HALF + 1, :], first)
        targets.append(first + within)
    target = jnp.concatenate(targets, axis=1)
    block = lax.broadcasted_iota(jnp.int32, (N_Z * BLK, PEERS * HALF), 0)
    block = (block ^ (FIRST_Z * BLK)).astype(F32)
    chosen = jnp.where(block == target, 1.0, 0.0).astype(BF16)
    parts = jnp.concatenate([parts_ref[peer, 0:HALF, :] for peer in range(PEERS)], axis=0)
    high, mid, low = split3(parts)
    both = jnp.dot(chosen, jnp.concatenate([high, mid], axis=1), preferred_element_type=F32)
    total = both[:, :LANES] + (both[:, LANES:] + jnp.dot(chosen, low, preferred_element_type=F32))
    out_ref[...] = total


def finish_kernel(parts_ref, out_ref):
    total = parts_ref[0]
    for z in range(1, N_Z):
        total = total + parts_ref[z]
    columns = pltpu.roll(total, SUB, 1)
    out_ref[...] = (total / jnp.maximum(columns, 1.0))[:, :SUB]


def call(kernel, out_shape, in_specs, scratch=(), cost=None, limit=16):
    return pl.pallas_call(
        kernel,
        out_shape=out_shape,
        in_specs=in_specs,
        out_specs=jax.tree.map(lambda _: VMEM, out_shape),
        scratch_shapes=scratch,
        cost_estimate=cost,
        compiler_params=pltpu.CompilerParams(vmem_limit_bytes=limit * 2**20),
    )


def shards(volume, footprint, offsets, ray_weights, measured):
    member = lax.axis_index("vol")
    core = member & 1
    swap = [(i, i ^ 1) for i in range(2 * N_Z)]
    chips = [[2 * (z ^ FIRST_Z) + c for z in range(N_Z)] for c in range(2)]
    planes = [[z * PEERS + (peer ^ FIRST_VIEW) for peer in range(PEERS)] for z in range(N_Z)]

    other = lax.ppermute(volume, "vol", swap)
    sent = call(
        pick_kernel,
        jax.ShapeDtypeStruct((N_Z, 4 * TILES, LANES), F32),
        [SMEM, HBM, HBM, VMEM],
        [
            pltpu.VMEM((2 * BLK * TILES, LANES), F32),
            pltpu.VMEM((BLK, VOXELS), F32),
            pltpu.SMEM((2 * N_Z, 1, FOOT), jnp.int32),
            pltpu.SemaphoreType.DMA((2,)),
        ],
    )(core[None], footprint, volume, other)
    blocks = lax.all_to_all(sent, "vol", 0, 0, axis_index_groups=chips)

    weights = ray_weights.reshape(8, 2, 2, BAND, FOLDS * VOXELS)
    weights = jnp.transpose(weights, (3, 1, 2, 0, 4)).reshape(BAND, FOOT, FOLDS * VOXELS)
    counts = jnp.transpose(offsets.reshape(8, 2, 2), (1, 2, 0)).reshape(FOOT, 1)
    counts = jnp.broadcast_to(counts, (FOOT, LANES))
    work = BAND * FOOT * FOLDS * VOXELS
    columns, turned, row_sum = call(
        sums_kernel,
        (
            jax.ShapeDtypeStruct((FOOT, VOXELS), F32),
            jax.ShapeDtypeStruct((FOOT, VOXELS), F32),
            jax.ShapeDtypeStruct((FOLDS, VOXELS), F32),
        ),
        [VMEM, VMEM],
        [pltpu.VMEM((BAND, FOOT, VOXELS), F32)],
        pl.CostEstimate(flops=2 * work, bytes_accessed=2 * work, transcendentals=0),
    )(weights, counts)

    first_block = lax.dynamic_index_in_dim(footprint[:, 0, 0], member, 0, keepdims=False)
    parts = call(
        rays_kernel,
        jax.ShapeDtypeStruct((PEERS, MSG, LANES), F32),
        [SMEM] + [VMEM] * 7,
        [
            pltpu.VMEM((BAND, FOOT, VOXELS), F32),
            pltpu.VMEM((BAND, FOOT, VOXELS), F32),
            pltpu.VMEM((FOLDS, VOXELS), F32),
        ],
        pl.CostEstimate(flops=4 * work, bytes_accessed=2 * work, transcendentals=0),
    )(
        jnp.stack([core, first_block]),
        blocks.reshape(N_Z * 4 * TILES, LANES),
        weights,
        counts,
        measured.reshape(FOLDS, VOXELS),
        row_sum,
        columns,
        turned,
    )
    parts = lax.all_to_all(parts, ("vol", "view"), 0, 0, axis_index_groups=planes)
    placed = call(place_kernel, jax.ShapeDtypeStruct((N_Z * BLK, LANES), F32), [VMEM])(parts)
    placed = lax.all_to_all(placed.reshape(N_Z, BLK, LANES), "vol", 0, 0, axis_index_groups=chips)
    return call(finish_kernel, jax.ShapeDtypeStruct((BLK, SUB), F32), [VMEM])(placed)


def solution(mesh):
    in_specs = (
        P("vol", None),
        P(None, "view", None),
        P("vol", "view", None),
        P("vol", "view", None, None, None),
        P("vol", "view", None),
    )
    return jax.shard_map(shards, mesh=mesh, in_specs=in_specs, out_specs=P("vol", "view"), check_vma=False)
```

```python
import jax
import jax.numpy as jnp
from jax import lax
from jax.experimental import pallas as pl
from jax.experimental.pallas import tpu as pltpu
from jax.sharding import PartitionSpec as P

VOXELS = 1024
LANES = 128
TILES = VOXELS // LANES
FOOT = 32
HALF = FOOT // 2
BAND = 4
FOLDS = 8
BLK = 8
N_Z = 16
N_VIEW = 16
PEERS = 2 * N_VIEW
MSG = HALF + 8
SUB = VOXELS // N_VIEW
FIRST_OUT = 11
FIRST_BACK = 8
FIRST_VIEW = 10

VMEM = pl.BlockSpec(memory_space=pltpu.VMEM)
SMEM = pl.BlockSpec(memory_space=pltpu.SMEM)
F32 = jnp.float32
BF16 = jnp.bfloat16


def lane_tiles(rows):
    return [rows[:, tile * LANES : (tile + 1) * LANES] for tile in range(TILES)]


def rotate_each(tiles, counts, left):
    lane = lax.broadcasted_iota(jnp.int32, (FOOT, LANES), 1)
    within = counts & (LANES - 1)
    source = (lane + within if left else lane - within) & (LANES - 1)
    same = lane + within < LANES if left else lane >= within
    step = 1 if left else TILES - 1
    moved = [jnp.take_along_axis(tile, source, axis=1) for tile in tiles]
    tiles = [jnp.where(same, moved[t], moved[(t + step) % TILES]) for t in range(TILES)]
    for bit in range(3):
        far = step << bit
        chosen = (counts >> (7 + bit)) & 1 == 1
        tiles = [jnp.where(chosen, tiles[(t + far) % TILES], tiles[t]) for t in range(TILES)]
    return tiles


def split3(x):
    high = x.astype(BF16)
    rest = x - high.astype(F32)
    mid = rest.astype(BF16)
    low = (rest - mid.astype(F32)).astype(BF16)
    return high, mid, low


def fold_lags(spread_ref, counts):
    total = spread_ref[BAND - 1]
    for lag in range(BAND - 2, -1, -1):
        total = pltpu.roll(total, 1, 1) + spread_ref[lag]
    return rotate_each(lane_tiles(total), counts, False)


def sum_rows(totals):
    row = lax.broadcasted_iota(jnp.int32, (8, LANES), 0)
    low = row < 4
    fours = [
        jnp.where(low, totals[k], totals[k + 4]) + pltpu.roll(jnp.where(low, totals[k + 4], totals[k]), 4, 0)
        for k in range(4)
    ]

    def halve(parts, width):
        first = row & width == 0
        count = len(parts) // 2
        return [
            jnp.where(
                first,
                parts[k] + pltpu.roll(parts[k], 8 - width, 0),
                parts[k + count] + pltpu.roll(parts[k + count], width, 0),
            )
            for k in range(count)
        ]

    return halve(halve(fours, 2), 1)[0]


def quarter(tile):
    return tile[0:8] + tile[8:16] + tile[16:24] + tile[24:32]


def lanes_of(fold, tile):
    if isinstance(tile, int):
        return slice(fold * VOXELS + tile * LANES, fold * VOXELS + (tile + 1) * LANES)
    return pl.ds(pl.multiple_of(fold * VOXELS + tile * LANES, LANES), LANES)


def spread_rows(rows_ref, ref):
    for tile in range(TILES):
        rows_ref[pl.ds(tile, BLK, stride=TILES), :] = ref[:, tile * LANES : (tile + 1) * LANES]


def own_kernel(core_ref, foot_ref, own_ref, half_ref, column_ref, rows_ref):
    core = core_ref[0]
    spread_rows(rows_ref, own_ref)
    for z in range(N_Z):
        column = foot_ref[2 * z + core, 0, 0] & (BLK - 1)
        place = (z - FIRST_OUT) % N_Z
        first = pl.multiple_of(column * TILES, TILES)
        half_ref[place] = rows_ref[pl.ds(first, 2 * TILES), :]
        column_ref[place] = jnp.full((TILES, LANES), column, jnp.int32)


def other_kernel(half_ref, column_ref, other_ref, sent_ref, rows_ref):
    spread_rows(rows_ref, other_ref)
    rows = [rows_ref[block * TILES : (block + 1) * TILES, :] for block in range(BLK)]
    for place in range(N_Z):
        column = column_ref[place]
        one, two = rows[0], rows[1]
        for block in range(1, BLK - 1):
            chosen = column == block
            one = jnp.where(chosen, rows[block], one)
            two = jnp.where(chosen, rows[block + 1], two)
        sent_ref[place, 0 : 2 * TILES, :] = half_ref[place]
        sent_ref[place, 2 * TILES : 3 * TILES, :] = one
        sent_ref[place, 3 * TILES : 4 * TILES, :] = two


def sums_kernel(weights_ref, counts_ref, column_ref, turned_ref, row_ref, spread_ref):
    def tile_step(tile, carry):
        spread = [jnp.zeros((FOOT, LANES), F32) for _ in range(BAND)]
        rows = []
        for fold in range(FOLDS):
            total = jnp.zeros((FOOT, LANES), F32)
            for lag in range(BAND):
                weights = weights_ref[lag, :, lanes_of(fold, tile)].astype(F32)
                spread[lag] = spread[lag] + weights
                total = total + weights
            rows.append(quarter(total))
        row_ref[:, lanes_of(0, tile)] = sum_rows(rows)
        for lag in range(BAND):
            spread_ref[lag, :, lanes_of(0, tile)] = spread[lag]
        return carry

    lax.fori_loop(0, TILES, tile_step, 0)
    for tile, columns in enumerate(fold_lags(spread_ref, counts_ref[...])):
        column_ref[:, tile * LANES : (tile + 1) * LANES] = columns
        turned_ref[:, tile * LANES : (tile + 1) * LANES] = pltpu.roll(columns, SUB, 1)


def rays_kernel(
    place_ref,
    blocks_ref,
    weights_ref,
    counts_ref,
    measured_ref,
    row_ref,
    column_ref,
    turned_ref,
    out_ref,
    window_ref,
    spread_ref,
    share_ref,
):
    core, first_block = place_ref[0], place_ref[1]
    first_owner = first_block >> 3
    odd = first_owner & 1
    double = 2 * ((lax.broadcasted_iota(jnp.int32, (8, LANES), 0) + FIRST_OUT) & (N_Z - 1))
    covered = [[] for _ in range(TILES)]
    for step in range(2):
        parity = step ^ odd
        side = parity ^ core
        owner = double + parity - first_owner
        near = (owner >= 0) & (owner < N_Z)
        turn = (FIRST_OUT - ((first_owner + 1 - parity) >> 1)) & 7
        for column in range(2):
            for tile in range(TILES):
                rows = blocks_ref[pl.ds((side * 2 + column) * TILES + tile, N_Z, stride=4 * TILES), :]
                covered[tile].append(pltpu.roll(jnp.where(near, rows[0:8], rows[8:16]), turn, 0))
    counts = counts_ref[...]
    window = jnp.concatenate(rotate_each([jnp.concatenate(c, axis=0) for c in covered], counts, True), axis=1)
    window_ref[0] = window
    for lag in range(1, BAND):
        window_ref[lag] = pltpu.roll(window, VOXELS - lag, 1)

    for tile in range(TILES):
        lanes = lanes_of(0, tile)
        windows = [window_ref[lag, :, lanes] for lag in range(BAND)]
        rows = []
        for fold in range(FOLDS):
            total = weights_ref[0, :, lanes_of(fold, tile)].astype(F32) * windows[0]
            for lag in range(1, BAND):
                total = total + weights_ref[lag, :, lanes_of(fold, tile)].astype(F32) * windows[lag]
            rows.append(quarter(total))
        share_ref[:, lanes] = (measured_ref[:, lanes] - sum_rows(rows)) / row_ref[:, lanes]
    for tile in range(TILES):
        lanes = lanes_of(0, tile)
        for lag in range(BAND):
            spread = weights_ref[lag, :, lanes].astype(F32) * share_ref[0:1, lanes]
            for fold in range(1, FOLDS):
                spread = spread + weights_ref[lag, :, lanes_of(fold, tile)].astype(F32) * share_ref[fold : fold + 1, lanes]
            spread_ref[lag, :, lanes] = spread
    low = lax.broadcasted_iota(jnp.int32, (HALF, LANES), 1) < SUB
    back = fold_lags(spread_ref, counts)
    for step in range(2):
        parity = step ^ odd
        first = parity * N_VIEW
        even = [first + (2 * tile ^ FIRST_VIEW) for tile in range(TILES)]
        other = [first + (2 * tile + 1 ^ FIRST_VIEW) for tile in range(TILES)]
        base = (((first_owner + 1 - parity) >> 1) << 3) + (first_block & 7)
        base = jnp.full((8, LANES), base, jnp.int32).astype(F32)
        part = slice(step * HALF, (step + 1) * HALF)
        for tile in range(TILES):
            lanes = slice(tile * LANES, (tile + 1) * LANES)
            sums = back[tile][part]
            out_ref[even[tile], 0:HALF, :] = jnp.where(low, sums, turned_ref[part, lanes])
            out_ref[other[tile], 0:HALF, :] = jnp.where(low, pltpu.roll(sums, SUB, 1), column_ref[part, lanes])
            out_ref[even[tile], HALF:MSG, :] = base
            out_ref[other[tile], HALF:MSG, :] = base


def place_kernel(parts_ref, out_ref):
    lane = lax.broadcasted_iota(jnp.int32, (1, LANES), 1)
    within = ((lane & 7) * BLK + ((lane >> 3) & 1)).astype(F32)
    source = lane >> 4
    targets = []
    for group in range(0, PEERS, 8):
        first = parts_ref[group, HALF : HALF + 1, :]
        for other in range(1, 8):
            first = jnp.where(source == other, parts_ref[group + other, HALF : HALF + 1, :], first)
        targets.append(first + within)
    target = jnp.concatenate(targets, axis=1)
    block = lax.broadcasted_iota(jnp.int32, (N_Z * BLK, PEERS * HALF), 0)
    block = ((block + FIRST_BACK * BLK) & (N_Z * BLK - 1)).astype(F32)
    chosen = jnp.where(block == target, 1.0, 0.0).astype(BF16)
    parts = jnp.concatenate([parts_ref[peer, 0:HALF, :] for peer in range(PEERS)], axis=0)
    high, mid, low = split3(parts)
    both = jnp.dot(chosen, jnp.concatenate([high, mid], axis=1), preferred_element_type=F32)
    total = both[:, :LANES] + (both[:, LANES:] + jnp.dot(chosen, low, preferred_element_type=F32))
    out_ref[...] = total


def finish_kernel(parts_ref, out_ref):
    total = parts_ref[0]
    for z in range(1, N_Z):
        total = total + parts_ref[z]
    columns = pltpu.roll(total, SUB, 1)
    out_ref[...] = (total / jnp.maximum(columns, 1.0))[:, :SUB]


def call(kernel, out_shape, in_specs, scratch=(), cost=None):
    return pl.pallas_call(
        kernel,
        out_shape=out_shape,
        in_specs=in_specs,
        out_specs=jax.tree.map(lambda _: VMEM, out_shape),
        scratch_shapes=scratch,
        cost_estimate=cost,
        compiler_params=pltpu.CompilerParams(vmem_limit_bytes=16 * 2**20),
    )


def shards(volume, footprint, offsets, ray_weights, measured):
    member = lax.axis_index("vol")
    core = member & 1
    swap = [(i, i ^ 1) for i in range(2 * N_Z)]
    out_chips, back_chips = (
        [[2 * ((z + first) % N_Z) + c for z in range(N_Z)] for c in range(2)] for first in (FIRST_OUT, FIRST_BACK)
    )
    planes = [[z * PEERS + (peer ^ FIRST_VIEW) for peer in range(PEERS)] for z in range(N_Z)]

    other = lax.ppermute(volume, "vol", swap)
    rows_scratch = pltpu.VMEM((BLK * TILES, LANES), F32)
    half, chosen = call(
        own_kernel,
        (
            jax.ShapeDtypeStruct((N_Z, 2 * TILES, LANES), F32),
            jax.ShapeDtypeStruct((N_Z, TILES, LANES), jnp.int32),
        ),
        [SMEM, SMEM, VMEM],
        [rows_scratch],
    )(core[None], footprint, volume)
    sent = call(
        other_kernel,
        jax.ShapeDtypeStruct((N_Z, 4 * TILES, LANES), F32),
        [VMEM] * 3,
        [rows_scratch],
    )(half, chosen, other)
    blocks = lax.all_to_all(sent, "vol", 0, 0, axis_index_groups=out_chips)

    weights = ray_weights.reshape(8, 2, 2, BAND, FOLDS * VOXELS)
    weights = jnp.transpose(weights, (3, 1, 2, 0, 4)).reshape(BAND, FOOT, FOLDS * VOXELS)
    counts = jnp.transpose(offsets.reshape(8, 2, 2), (1, 2, 0)).reshape(FOOT, 1)
    counts = jnp.broadcast_to(counts, (FOOT, LANES))
    work = BAND * FOOT * FOLDS * VOXELS
    columns, turned, row_sum = call(
        sums_kernel,
        (
            jax.ShapeDtypeStruct((FOOT, VOXELS), F32),
            jax.ShapeDtypeStruct((FOOT, VOXELS), F32),
            jax.ShapeDtypeStruct((FOLDS, VOXELS), F32),
        ),
        [VMEM, VMEM],
        [pltpu.VMEM((BAND, FOOT, VOXELS), F32)],
        pl.CostEstimate(flops=2 * work, bytes_accessed=2 * work, transcendentals=0),
    )(weights, counts)

    first_block = lax.dynamic_index_in_dim(footprint[:, 0, 0], member, 0, keepdims=False)
    parts = call(
        rays_kernel,
        jax.ShapeDtypeStruct((PEERS, MSG, LANES), F32),
        [SMEM] + [VMEM] * 7,
        [
            pltpu.VMEM((BAND, FOOT, VOXELS), F32),
            pltpu.VMEM((BAND, FOOT, VOXELS), F32),
            pltpu.VMEM((FOLDS, VOXELS), F32),
        ],
        pl.CostEstimate(flops=4 * work, bytes_accessed=2 * work, transcendentals=0),
    )(
        jnp.stack([core, first_block]),
        blocks.reshape(N_Z * 4 * TILES, LANES),
        weights,
        counts,
        measured.reshape(FOLDS, VOXELS),
        row_sum,
        columns,
        turned,
    )
    parts = lax.all_to_all(parts, ("vol", "view"), 0, 0, axis_index_groups=planes)
    placed = call(place_kernel, jax.ShapeDtypeStruct((N_Z * BLK, LANES), F32), [VMEM])(parts)
    placed = lax.all_to_all(placed.reshape(N_Z, BLK, LANES), "vol", 0, 0, axis_index_groups=back_chips)
    return call(finish_kernel, jax.ShapeDtypeStruct((BLK, SUB), F32), [VMEM])(placed)


def solution(mesh):
    in_specs = (
        P("vol", None),
        P(None, "view", None),
        P("vol", "view", None),
        P("vol", "view", None, None, None),
        P("vol", "view", None),
    )
    return jax.shard_map(shards, mesh=mesh, in_specs=in_specs, out_specs=P("vol", "view"), check_vma=False)
```

```python
import jax
import jax.numpy as jnp
from jax import lax
from jax.experimental import pallas as pl
from jax.experimental.pallas import tpu as pltpu
from jax.sharding import PartitionSpec as P

VOXELS = 1024
LANES = 128
TILES = VOXELS // LANES
FOOT = 32
HALF = FOOT // 2
BAND = 4
FOLDS = 8
BLK = 8
N_Z = 16
N_VIEW = 16
PEERS = 2 * N_VIEW
MSG = HALF + 8
SUB = VOXELS // N_VIEW
FIRST_OUT = 11
FIRST_BACK = 9
FIRST_VIEW = 10

VMEM = pl.BlockSpec(memory_space=pltpu.VMEM)
SMEM = pl.BlockSpec(memory_space=pltpu.SMEM)
F32 = jnp.float32
BF16 = jnp.bfloat16


def lane_tiles(rows):
    return [rows[:, tile * LANES : (tile + 1) * LANES] for tile in range(TILES)]


def rotate_each(tiles, counts, left):
    lane = lax.broadcasted_iota(jnp.int32, (FOOT, LANES), 1)
    within = counts & (LANES - 1)
    source = (lane + within if left else lane - within) & (LANES - 1)
    same = lane + within < LANES if left else lane >= within
    step = 1 if left else TILES - 1
    moved = [jnp.take_along_axis(tile, source, axis=1) for tile in tiles]
    tiles = [jnp.where(same, moved[t], moved[(t + step) % TILES]) for t in range(TILES)]
    for bit in range(3):
        far = step << bit
        chosen = (counts >> (7 + bit)) & 1 == 1
        tiles = [jnp.where(chosen, tiles[(t + far) % TILES], tiles[t]) for t in range(TILES)]
    return tiles


def split3(x):
    high = x.astype(BF16)
    rest = x - high.astype(F32)
    mid = rest.astype(BF16)
    low = (rest - mid.astype(F32)).astype(BF16)
    return high, mid, low


def fold_lags(spread_ref, counts):
    total = spread_ref[BAND - 1]
    for lag in range(BAND - 2, -1, -1):
        total = pltpu.roll(total, 1, 1) + spread_ref[lag]
    return rotate_each(lane_tiles(total), counts, False)


def sum_rows(totals):
    row = lax.broadcasted_iota(jnp.int32, (8, LANES), 0)
    low = row < 4
    fours = [
        jnp.where(low, totals[k], totals[k + 4]) + pltpu.roll(jnp.where(low, totals[k + 4], totals[k]), 4, 0)
        for k in range(4)
    ]

    def halve(parts, width):
        first = row & width == 0
        count = len(parts) // 2
        return [
            jnp.where(
                first,
                parts[k] + pltpu.roll(parts[k], 8 - width, 0),
                parts[k + count] + pltpu.roll(parts[k + count], width, 0),
            )
            for k in range(count)
        ]

    return halve(halve(fours, 2), 1)[0]


def quarter(tile):
    return tile[0:8] + tile[8:16] + tile[16:24] + tile[24:32]


def lanes_of(fold, tile):
    if isinstance(tile, int):
        return slice(fold * VOXELS + tile * LANES, fold * VOXELS + (tile + 1) * LANES)
    return pl.ds(pl.multiple_of(fold * VOXELS + tile * LANES, LANES), LANES)


def pick_pairs(rows_ref, column_ref, out_ref, first):
    rows = [rows_ref[block * TILES : (block + 1) * TILES, :] for block in range(BLK)]
    for place in range(N_Z):
        column = column_ref[place]
        one, two = rows[0], rows[1]
        for block in range(1, BLK - 1):
            chosen = column == block
            one = jnp.where(chosen, rows[block], one)
            two = jnp.where(chosen, rows[block + 1], two)
        out_ref[place, first : first + TILES, :] = one
        out_ref[place, first + TILES : first + 2 * TILES, :] = two


def own_kernel(core_ref, foot_ref, own_ref, half_ref, column_ref, rows_ref):
    core = core_ref[0]
    for z in range(N_Z):
        place = (z - FIRST_OUT) % N_Z
        first = foot_ref[2 * z + core] & (BLK - 1)
        column_ref[place] = jnp.broadcast_to(first[:, 0:1], (TILES, LANES))
    for tile in range(TILES):
        rows_ref[pl.ds(tile, BLK, stride=TILES), :] = own_ref[:, tile * LANES : (tile + 1) * LANES]
    pick_pairs(rows_ref, column_ref, half_ref, 0)


def other_kernel(half_ref, column_ref, other_ref, sent_ref, rows_ref):
    for tile in range(TILES):
        rows_ref[pl.ds(tile, BLK, stride=TILES), :] = other_ref[:, tile * LANES : (tile + 1) * LANES]
    for place in range(N_Z):
        sent_ref[place, 0 : 2 * TILES, :] = half_ref[place]
    pick_pairs(rows_ref, column_ref, sent_ref, 2 * TILES)


def sums_kernel(weights_ref, counts_ref, column_ref, turned_ref, row_ref, spread_ref):
    def tile_step(tile, carry):
        spread = [jnp.zeros((FOOT, LANES), F32) for _ in range(BAND)]
        rows = []
        for fold in range(FOLDS):
            total = jnp.zeros((FOOT, LANES), F32)
            for lag in range(BAND):
                weights = weights_ref[lag, :, lanes_of(fold, tile)].astype(F32)
                spread[lag] = spread[lag] + weights
                total = total + weights
            rows.append(quarter(total))
        row_ref[:, lanes_of(0, tile)] = sum_rows(rows)
        for lag in range(BAND):
            spread_ref[lag, :, lanes_of(0, tile)] = spread[lag]
        return carry

    lax.fori_loop(0, TILES, tile_step, 0)
    for tile, columns in enumerate(fold_lags(spread_ref, counts_ref[...])):
        column_ref[:, tile * LANES : (tile + 1) * LANES] = columns
        turned_ref[:, tile * LANES : (tile + 1) * LANES] = pltpu.roll(columns, SUB, 1)


def rays_kernel(
    place_ref,
    blocks_ref,
    weights_ref,
    counts_ref,
    measured_ref,
    row_ref,
    column_ref,
    turned_ref,
    out_ref,
    window_ref,
    spread_ref,
    share_ref,
):
    core, first_block = place_ref[0], place_ref[1]
    first_owner = first_block >> 3
    odd = first_owner & 1
    double = 2 * ((lax.broadcasted_iota(jnp.int32, (8, LANES), 0) + FIRST_OUT) & (N_Z - 1))
    covered = [[] for _ in range(TILES)]
    for step in range(2):
        parity = step ^ odd
        side = parity ^ core
        owner = double + parity - first_owner
        near = (owner >= 0) & (owner < N_Z)
        turn = (FIRST_OUT - ((first_owner + 1 - parity) >> 1)) & 7
        for column in range(2):
            for tile in range(TILES):
                rows = blocks_ref[pl.ds((side * 2 + column) * TILES + tile, N_Z, stride=4 * TILES), :]
                covered[tile].append(pltpu.roll(jnp.where(near, rows[0:8], rows[8:16]), turn, 0))
    counts = counts_ref[...]
    window = jnp.concatenate(rotate_each([jnp.concatenate(c, axis=0) for c in covered], counts, True), axis=1)
    window_ref[0] = window
    for lag in range(1, BAND):
        window_ref[lag] = pltpu.roll(window, VOXELS - lag, 1)

    for tile in range(TILES):
        lanes = lanes_of(0, tile)
        windows = [window_ref[lag, :, lanes] for lag in range(BAND)]
        rows = []
        for fold in range(FOLDS):
            total = weights_ref[0, :, lanes_of(fold, tile)].astype(F32) * windows[0]
            for lag in range(1, BAND):
                total = total + weights_ref[lag, :, lanes_of(fold, tile)].astype(F32) * windows[lag]
            rows.append(quarter(total))
        share_ref[:, lanes] = (measured_ref[:, lanes] - sum_rows(rows)) / row_ref[:, lanes]
    for tile in range(TILES):
        lanes = lanes_of(0, tile)
        for lag in range(BAND):
            spread = weights_ref[lag, :, lanes].astype(F32) * share_ref[0:1, lanes]
            for fold in range(1, FOLDS):
                spread = spread + weights_ref[lag, :, lanes_of(fold, tile)].astype(F32) * share_ref[fold : fold + 1, lanes]
            spread_ref[lag, :, lanes] = spread
    low = lax.broadcasted_iota(jnp.int32, (HALF, LANES), 1) < SUB
    back = fold_lags(spread_ref, counts)
    for step in range(2):
        parity = step ^ odd
        first = parity * N_VIEW
        even = [first + (2 * tile ^ FIRST_VIEW) for tile in range(TILES)]
        other = [first + (2 * tile + 1 ^ FIRST_VIEW) for tile in range(TILES)]
        base = (((first_owner + 1 - parity) >> 1) << 3) + (first_block & 7)
        base = jnp.full((8, LANES), base, jnp.int32).astype(F32)
        part = slice(step * HALF, (step + 1) * HALF)
        for tile in range(TILES):
            lanes = slice(tile * LANES, (tile + 1) * LANES)
            sums = back[tile][part]
            out_ref[even[tile], 0:HALF, :] = jnp.where(low, sums, turned_ref[part, lanes])
            out_ref[other[tile], 0:HALF, :] = jnp.where(low, pltpu.roll(sums, SUB, 1), column_ref[part, lanes])
            out_ref[even[tile], HALF:MSG, :] = base
            out_ref[other[tile], HALF:MSG, :] = base


def place_kernel(parts_ref, out_ref):
    lane = lax.broadcasted_iota(jnp.int32, (1, LANES), 1)
    within = ((lane & 7) * BLK + ((lane >> 3) & 1)).astype(F32)
    source = lane >> 4
    targets = []
    for group in range(0, PEERS, 8):
        first = parts_ref[group, HALF : HALF + 1, :]
        for other in range(1, 8):
            first = jnp.where(source == other, parts_ref[group + other, HALF : HALF + 1, :], first)
        targets.append(first + within)
    target = jnp.concatenate(targets, axis=1)
    block = lax.broadcasted_iota(jnp.int32, (N_Z * BLK, PEERS * HALF), 0)
    block = ((block + FIRST_BACK * BLK) & (N_Z * BLK - 1)).astype(F32)
    chosen = jnp.where(block == target, 1.0, 0.0).astype(BF16)
    parts = jnp.concatenate([parts_ref[peer, 0:HALF, :] for peer in range(PEERS)], axis=0)
    high, mid, low = split3(parts)
    both = jnp.dot(chosen, jnp.concatenate([high, mid], axis=1), preferred_element_type=F32)
    total = both[:, :LANES] + (both[:, LANES:] + jnp.dot(chosen, low, preferred_element_type=F32))
    out_ref[...] = total


def finish_kernel(parts_ref, out_ref):
    total = parts_ref[0]
    for z in range(1, N_Z):
        total = total + parts_ref[z]
    columns = pltpu.roll(total, SUB, 1)
    out_ref[...] = (total / jnp.maximum(columns, 1.0))[:, :SUB]


def call(kernel, out_shape, in_specs, scratch=(), cost=None):
    return pl.pallas_call(
        kernel,
        out_shape=out_shape,
        in_specs=in_specs,
        out_specs=jax.tree.map(lambda _: VMEM, out_shape),
        scratch_shapes=scratch,
        cost_estimate=cost,
        compiler_params=pltpu.CompilerParams(vmem_limit_bytes=16 * 2**20),
    )


def shards(volume, footprint, offsets, ray_weights, measured):
    member = lax.axis_index("vol")
    core = member & 1
    swap = [(i, i ^ 1) for i in range(2 * N_Z)]
    out_chips, back_chips = (
        [[2 * ((z + first) % N_Z) + c for z in range(N_Z)] for c in range(2)] for first in (FIRST_OUT, FIRST_BACK)
    )
    planes = [[z * PEERS + (peer ^ FIRST_VIEW) for peer in range(PEERS)] for z in range(N_Z)]

    other = lax.ppermute(volume, "vol", swap)
    rows_scratch = pltpu.VMEM((BLK * TILES, LANES), F32)
    half, chosen = call(
        own_kernel,
        (
            jax.ShapeDtypeStruct((N_Z, 2 * TILES, LANES), F32),
            jax.ShapeDtypeStruct((N_Z, TILES, LANES), jnp.int32),
        ),
        [SMEM, VMEM, VMEM],
        [rows_scratch],
    )(core[None], footprint, volume)
    sent = call(
        other_kernel,
        jax.ShapeDtypeStruct((N_Z, 4 * TILES, LANES), F32),
        [VMEM] * 3,
        [rows_scratch],
    )(half, chosen, other)
    blocks = lax.all_to_all(sent, "vol", 0, 0, axis_index_groups=out_chips)

    weights = ray_weights.reshape(8, 2, 2, BAND, FOLDS * VOXELS)
    weights = jnp.transpose(weights, (3, 1, 2, 0, 4)).reshape(BAND, FOOT, FOLDS * VOXELS)
    counts = jnp.transpose(offsets.reshape(8, 2, 2), (1, 2, 0)).reshape(FOOT, 1)
    counts = jnp.broadcast_to(counts, (FOOT, LANES))
    work = BAND * FOOT * FOLDS * VOXELS
    columns, turned, row_sum = call(
        sums_kernel,
        (
            jax.ShapeDtypeStruct((FOOT, VOXELS), F32),
            jax.ShapeDtypeStruct((FOOT, VOXELS), F32),
            jax.ShapeDtypeStruct((FOLDS, VOXELS), F32),
        ),
        [VMEM, VMEM],
        [pltpu.VMEM((BAND, FOOT, VOXELS), F32)],
        pl.CostEstimate(flops=2 * work, bytes_accessed=2 * work, transcendentals=0),
    )(weights, counts)

    first_block = lax.dynamic_index_in_dim(footprint[:, 0, 0], member, 0, keepdims=False)
    parts = call(
        rays_kernel,
        jax.ShapeDtypeStruct((PEERS, MSG, LANES), F32),
        [SMEM] + [VMEM] * 7,
        [
            pltpu.VMEM((BAND, FOOT, VOXELS), F32),
            pltpu.VMEM((BAND, FOOT, VOXELS), F32),
            pltpu.VMEM((FOLDS, VOXELS), F32),
        ],
        pl.CostEstimate(flops=4 * work, bytes_accessed=2 * work, transcendentals=0),
    )(
        jnp.stack([core, first_block]),
        blocks.reshape(N_Z * 4 * TILES, LANES),
        weights,
        counts,
        measured.reshape(FOLDS, VOXELS),
        row_sum,
        columns,
        turned,
    )
    parts = lax.all_to_all(parts, ("vol", "view"), 0, 0, axis_index_groups=planes)
    placed = call(place_kernel, jax.ShapeDtypeStruct((N_Z * BLK, LANES), F32), [VMEM])(parts)
    placed = lax.all_to_all(placed.reshape(N_Z, BLK, LANES), "vol", 0, 0, axis_index_groups=back_chips)
    return call(finish_kernel, jax.ShapeDtypeStruct((BLK, SUB), F32), [VMEM])(placed)


def solution(mesh):
    in_specs = (
        P("vol", None),
        P(None, "view", None),
        P("vol", "view", None),
        P("vol", "view", None, None, None),
        P("vol", "view", None),
    )
    return jax.shard_map(shards, mesh=mesh, in_specs=in_specs, out_specs=P("vol", "view"), check_vma=False)
```

```python
import jax
import jax.numpy as jnp
from jax import lax
from jax.experimental import pallas as pl
from jax.experimental.pallas import tpu as pltpu
from jax.sharding import PartitionSpec as P

VOXELS = 1024
LANES = 128
TILES = VOXELS // LANES
FOOT = 32
HALF = FOOT // 2
BAND = 4
FOLDS = 8
BLK = 8
N_Z = 16
N_VIEW = 16
PEERS = 2 * N_VIEW
PIECE = 2
PIECES = HALF // PIECE
SUB = VOXELS // N_VIEW
FIRST_OUT = 11
FIRST_BACK = 9
FIRST_VIEW = 10
STEP_OUT = 9
STEP_BACK = 1

VMEM = pl.BlockSpec(memory_space=pltpu.VMEM)
SMEM = pl.BlockSpec(memory_space=pltpu.SMEM)
F32 = jnp.float32
BF16 = jnp.bfloat16


def lane_tiles(rows):
    return [rows[:, tile * LANES : (tile + 1) * LANES] for tile in range(TILES)]


def rotate_each(tiles, counts, left):
    lane = lax.broadcasted_iota(jnp.int32, (FOOT, LANES), 1)
    within = counts & (LANES - 1)
    source = (lane + within if left else lane - within) & (LANES - 1)
    same = lane + within < LANES if left else lane >= within
    step = 1 if left else TILES - 1
    moved = [jnp.take_along_axis(tile, source, axis=1) for tile in tiles]
    tiles = [jnp.where(same, moved[t], moved[(t + step) % TILES]) for t in range(TILES)]
    for bit in range(3):
        far = step << bit
        chosen = (counts >> (7 + bit)) & 1 == 1
        tiles = [jnp.where(chosen, tiles[(t + far) % TILES], tiles[t]) for t in range(TILES)]
    return tiles


def split3(x):
    high = x.astype(BF16)
    rest = x - high.astype(F32)
    mid = rest.astype(BF16)
    low = (rest - mid.astype(F32)).astype(BF16)
    return high, mid, low


def fold_lags(spread_ref, counts):
    total = spread_ref[BAND - 1]
    for lag in range(BAND - 2, -1, -1):
        total = pltpu.roll(total, 1, 1) + spread_ref[lag]
    return rotate_each(lane_tiles(total), counts, False)


def sum_rows(totals):
    row = lax.broadcasted_iota(jnp.int32, (8, LANES), 0)
    low = row < 4
    fours = [
        jnp.where(low, totals[k], totals[k + 4]) + pltpu.roll(jnp.where(low, totals[k + 4], totals[k]), 4, 0)
        for k in range(4)
    ]

    def halve(parts, width):
        first = row & width == 0
        count = len(parts) // 2
        return [
            jnp.where(
                first,
                parts[k] + pltpu.roll(parts[k], 8 - width, 0),
                parts[k + count] + pltpu.roll(parts[k + count], width, 0),
            )
            for k in range(count)
        ]

    return halve(halve(fours, 2), 1)[0]


def quarter(tile):
    return tile[0:8] + tile[8:16] + tile[16:24] + tile[24:32]


def lanes_of(fold, tile):
    if isinstance(tile, int):
        return slice(fold * VOXELS + tile * LANES, fold * VOXELS + (tile + 1) * LANES)
    return pl.ds(pl.multiple_of(fold * VOXELS + tile * LANES, LANES), LANES)


def pick_pairs(rows_ref, column_ref, out_ref, first):
    rows = [rows_ref[block * TILES : (block + 1) * TILES, :] for block in range(BLK)]
    for place in range(N_Z):
        column = column_ref[place]
        one, two = rows[0], rows[1]
        for block in range(1, BLK - 1):
            chosen = column == block
            one = jnp.where(chosen, rows[block], one)
            two = jnp.where(chosen, rows[block + 1], two)
        out_ref[place, first : first + TILES, :] = one
        out_ref[place, first + TILES : first + 2 * TILES, :] = two


def own_kernel(core_ref, foot_ref, own_ref, half_ref, column_ref, rows_ref):
    core = core_ref[0]
    for z in range(N_Z):
        place = STEP_OUT * (z - FIRST_OUT) % N_Z
        first = foot_ref[2 * z + core] & (BLK - 1)
        column_ref[place] = jnp.broadcast_to(first[:, 0:1], (TILES, LANES))
    for tile in range(TILES):
        rows_ref[pl.ds(tile, BLK, stride=TILES), :] = own_ref[:, tile * LANES : (tile + 1) * LANES]
    pick_pairs(rows_ref, column_ref, half_ref, 0)


def other_kernel(half_ref, column_ref, other_ref, sent_ref, rows_ref):
    for tile in range(TILES):
        rows_ref[pl.ds(tile, BLK, stride=TILES), :] = other_ref[:, tile * LANES : (tile + 1) * LANES]
    for place in range(N_Z):
        sent_ref[place, 0 : 2 * TILES, :] = half_ref[place]
    pick_pairs(rows_ref, column_ref, sent_ref, 2 * TILES)


def sums_kernel(weights_ref, counts_ref, column_ref, turned_ref, row_ref, spread_ref):
    def tile_step(tile, carry):
        spread = [jnp.zeros((FOOT, LANES), F32) for _ in range(BAND)]
        rows = []
        for fold in range(FOLDS):
            total = jnp.zeros((FOOT, LANES), F32)
            for lag in range(BAND):
                weights = weights_ref[lag, :, lanes_of(fold, tile)].astype(F32)
                spread[lag] = spread[lag] + weights
                total = total + weights
            rows.append(quarter(total))
        row_ref[:, lanes_of(0, tile)] = sum_rows(rows)
        for lag in range(BAND):
            spread_ref[lag, :, lanes_of(0, tile)] = spread[lag]
        return carry

    lax.fori_loop(0, TILES, tile_step, 0)
    for tile, columns in enumerate(fold_lags(spread_ref, counts_ref[...])):
        column_ref[:, tile * LANES : (tile + 1) * LANES] = columns
        turned_ref[:, tile * LANES : (tile + 1) * LANES] = pltpu.roll(columns, SUB, 1)


def message(out_ref, peer, rows, base):
    for piece in range(PIECES):
        out_ref[peer, piece] = rows[piece * PIECE : (piece + 1) * PIECE]
    out_ref[peer, PIECES] = base


def rays_kernel(
    place_ref,
    blocks_ref,
    weights_ref,
    counts_ref,
    measured_ref,
    row_ref,
    column_ref,
    turned_ref,
    out_ref,
    window_ref,
    spread_ref,
    share_ref,
):
    core, first_block = place_ref[0], place_ref[1]
    first_owner = first_block >> 3
    odd = first_owner & 1
    double = 2 * ((lax.broadcasted_iota(jnp.int32, (8, LANES), 0) * STEP_OUT + FIRST_OUT) & (N_Z - 1))
    covered = [[] for _ in range(TILES)]
    for step in range(2):
        parity = step ^ odd
        side = parity ^ core
        owner = double + parity - first_owner
        near = (owner >= 0) & (owner < N_Z)
        turn = (FIRST_OUT - ((first_owner + 1 - parity) >> 1)) & 7
        for column in range(2):
            for tile in range(TILES):
                rows = blocks_ref[pl.ds((side * 2 + column) * TILES + tile, N_Z, stride=4 * TILES), :]
                covered[tile].append(pltpu.roll(jnp.where(near, rows[0:8], rows[8:16]), turn, 0))
    counts = counts_ref[...]
    window = jnp.concatenate(rotate_each([jnp.concatenate(c, axis=0) for c in covered], counts, True), axis=1)
    window_ref[0] = window
    for lag in range(1, BAND):
        window_ref[lag] = pltpu.roll(window, VOXELS - lag, 1)

    for tile in range(TILES):
        lanes = lanes_of(0, tile)
        windows = [window_ref[lag, :, lanes] for lag in range(BAND)]
        rows = []
        for fold in range(FOLDS):
            total = weights_ref[0, :, lanes_of(fold, tile)].astype(F32) * windows[0]
            for lag in range(1, BAND):
                total = total + weights_ref[lag, :, lanes_of(fold, tile)].astype(F32) * windows[lag]
            rows.append(quarter(total))
        share_ref[:, lanes] = (measured_ref[:, lanes] - sum_rows(rows)) / row_ref[:, lanes]
    for tile in range(TILES):
        lanes = lanes_of(0, tile)
        for lag in range(BAND):
            spread = weights_ref[lag, :, lanes].astype(F32) * share_ref[0:1, lanes]
            for fold in range(1, FOLDS):
                spread = spread + weights_ref[lag, :, lanes_of(fold, tile)].astype(F32) * share_ref[fold : fold + 1, lanes]
            spread_ref[lag, :, lanes] = spread
    low = lax.broadcasted_iota(jnp.int32, (HALF, LANES), 1) < SUB
    back = fold_lags(spread_ref, counts)
    for step in range(2):
        parity = step ^ odd
        first = parity * N_VIEW
        even = [first + (2 * tile ^ FIRST_VIEW) for tile in range(TILES)]
        other = [first + (2 * tile + 1 ^ FIRST_VIEW) for tile in range(TILES)]
        base = (((first_owner + 1 - parity) >> 1) << 3) + (first_block & 7)
        base = jnp.full((PIECE, LANES), base, jnp.int32).astype(F32)
        part = slice(step * HALF, (step + 1) * HALF)
        for tile in range(TILES):
            lanes = slice(tile * LANES, (tile + 1) * LANES)
            sums = back[tile][part]
            message(out_ref, even[tile], jnp.where(low, sums, turned_ref[part, lanes]), base)
            message(out_ref, other[tile], jnp.where(low, pltpu.roll(sums, SUB, 1), column_ref[part, lanes]), base)


def place_kernel(parts_ref, out_ref):
    lane = lax.broadcasted_iota(jnp.int32, (1, LANES), 1)
    within = ((lane & 7) * BLK + ((lane >> 3) & 1)).astype(F32)
    source = lane >> 4
    targets = []
    for group in range(0, PEERS, 8):
        first = parts_ref[group, PIECES, 0:1, :]
        for other in range(1, 8):
            first = jnp.where(source == other, parts_ref[group + other, PIECES, 0:1, :], first)
        targets.append(first + within)
    target = jnp.concatenate(targets, axis=1)
    block = lax.broadcasted_iota(jnp.int32, (N_Z * BLK, PEERS * HALF), 0)
    chip = ((block >> 3) * STEP_BACK + FIRST_BACK) & (N_Z - 1)
    block = (chip * BLK + (block & (BLK - 1))).astype(F32)
    chosen = jnp.where(block == target, 1.0, 0.0).astype(BF16)
    parts = jnp.concatenate([parts_ref[peer, piece] for peer in range(PEERS) for piece in range(PIECES)], axis=0)
    high, mid, low = split3(parts)
    both = jnp.dot(chosen, jnp.concatenate([high, mid], axis=1), preferred_element_type=F32)
    total = both[:, :LANES] + (both[:, LANES:] + jnp.dot(chosen, low, preferred_element_type=F32))
    out_ref[...] = total


def finish_kernel(parts_ref, out_ref):
    total = parts_ref[0]
    for z in range(1, N_Z):
        total = total + parts_ref[z]
    columns = pltpu.roll(total, SUB, 1)
    out_ref[...] = (total / jnp.maximum(columns, 1.0))[:, :SUB]


def call(kernel, out_shape, in_specs, scratch=(), cost=None):
    return pl.pallas_call(
        kernel,
        out_shape=out_shape,
        in_specs=in_specs,
        out_specs=jax.tree.map(lambda _: VMEM, out_shape),
        scratch_shapes=scratch,
        cost_estimate=cost,
        compiler_params=pltpu.CompilerParams(vmem_limit_bytes=16 * 2**20),
    )


def shards(volume, footprint, offsets, ray_weights, measured):
    member = lax.axis_index("vol")
    core = member & 1
    swap = [(i, i ^ 1) for i in range(2 * N_Z)]
    out_chips, back_chips = (
        [[2 * ((step * place + first) % N_Z) + c for place in range(N_Z)] for c in range(2)]
        for first, step in ((FIRST_OUT, STEP_OUT), (FIRST_BACK, STEP_BACK))
    )
    planes = [[z * PEERS + (peer ^ FIRST_VIEW) for peer in range(PEERS)] for z in range(N_Z)]

    other = lax.ppermute(volume, "vol", swap)
    rows_scratch = pltpu.VMEM((BLK * TILES, LANES), F32)
    half, chosen = call(
        own_kernel,
        (
            jax.ShapeDtypeStruct((N_Z, 2 * TILES, LANES), F32),
            jax.ShapeDtypeStruct((N_Z, TILES, LANES), jnp.int32),
        ),
        [SMEM, VMEM, VMEM],
        [rows_scratch],
    )(core[None], footprint, volume)
    sent = call(
        other_kernel,
        jax.ShapeDtypeStruct((N_Z, 4 * TILES, LANES), F32),
        [VMEM] * 3,
        [rows_scratch],
    )(half, chosen, other)
    blocks = lax.all_to_all(sent, "vol", 0, 0, axis_index_groups=out_chips)

    weights = ray_weights.reshape(8, 2, 2, BAND, FOLDS * VOXELS)
    weights = jnp.transpose(weights, (3, 1, 2, 0, 4)).reshape(BAND, FOOT, FOLDS * VOXELS)
    counts = jnp.transpose(offsets.reshape(8, 2, 2), (1, 2, 0)).reshape(FOOT, 1)
    counts = jnp.broadcast_to(counts, (FOOT, LANES))
    work = BAND * FOOT * FOLDS * VOXELS
    columns, turned, row_sum = call(
        sums_kernel,
        (
            jax.ShapeDtypeStruct((FOOT, VOXELS), F32),
            jax.ShapeDtypeStruct((FOOT, VOXELS), F32),
            jax.ShapeDtypeStruct((FOLDS, VOXELS), F32),
        ),
        [VMEM, VMEM],
        [pltpu.VMEM((BAND, FOOT, VOXELS), F32)],
        pl.CostEstimate(flops=2 * work, bytes_accessed=2 * work, transcendentals=0),
    )(weights, counts)

    first_block = lax.dynamic_index_in_dim(footprint[:, 0, 0], member, 0, keepdims=False)
    parts = call(
        rays_kernel,
        jax.ShapeDtypeStruct((PEERS, PIECES + 1, PIECE, LANES), F32),
        [SMEM] + [VMEM] * 7,
        [
            pltpu.VMEM((BAND, FOOT, VOXELS), F32),
            pltpu.VMEM((BAND, FOOT, VOXELS), F32),
            pltpu.VMEM((FOLDS, VOXELS), F32),
        ],
        pl.CostEstimate(flops=4 * work, bytes_accessed=2 * work, transcendentals=0),
    )(
        jnp.stack([core, first_block]),
        blocks.reshape(N_Z * 4 * TILES, LANES),
        weights,
        counts,
        measured.reshape(FOLDS, VOXELS),
        row_sum,
        columns,
        turned,
    )
    parts = lax.all_to_all(parts, ("vol", "view"), 0, 0, axis_index_groups=planes)
    placed = call(place_kernel, jax.ShapeDtypeStruct((N_Z * BLK, LANES), F32), [VMEM])(parts)
    placed = lax.all_to_all(placed.reshape(N_Z, BLK, LANES), "vol", 0, 0, axis_index_groups=back_chips)
    return call(finish_kernel, jax.ShapeDtypeStruct((BLK, SUB), F32), [VMEM])(placed)


def solution(mesh):
    in_specs = (
        P("vol", None),
        P(None, "view", None),
        P("vol", "view", None),
        P("vol", "view", None, None, None),
        P("vol", "view", None),
    )
    return jax.shard_map(shards, mesh=mesh, in_specs=in_specs, out_specs=P("vol", "view"), check_vma=False)
```

```python
import jax
import jax.numpy as jnp
from jax import lax
from jax.experimental import pallas as pl
from jax.experimental.pallas import tpu as pltpu
from jax.sharding import PartitionSpec as P

VOXELS = 1024
LANES = 128
TILES = VOXELS // LANES
FOOT = 32
HALF = FOOT // 2
BAND = 4
FOLDS = 8
BLK = 8
N_Z = 16
N_VIEW = 16
PEERS = 2 * N_VIEW
PIECE = 1
PIECES = HALF // PIECE
SUB = VOXELS // N_VIEW
FIRST_OUT = 11
FIRST_BACK = 9
FIRST_VIEW = 10
STEP_OUT = 9
STEP_BACK = 1

VMEM = pl.BlockSpec(memory_space=pltpu.VMEM)
SMEM = pl.BlockSpec(memory_space=pltpu.SMEM)
F32 = jnp.float32
BF16 = jnp.bfloat16


def lane_tiles(rows):
    return [rows[:, tile * LANES : (tile + 1) * LANES] for tile in range(TILES)]


def rotate_each(tiles, counts, left):
    lane = lax.broadcasted_iota(jnp.int32, (FOOT, LANES), 1)
    within = counts & (LANES - 1)
    source = (lane + within if left else lane - within) & (LANES - 1)
    same = lane + within < LANES if left else lane >= within
    step = 1 if left else TILES - 1
    moved = [jnp.take_along_axis(tile, source, axis=1) for tile in tiles]
    tiles = [jnp.where(same, moved[t], moved[(t + step) % TILES]) for t in range(TILES)]
    for bit in range(3):
        far = step << bit
        chosen = (counts >> (7 + bit)) & 1 == 1
        tiles = [jnp.where(chosen, tiles[(t + far) % TILES], tiles[t]) for t in range(TILES)]
    return tiles


def split3(x):
    high = x.astype(BF16)
    rest = x - high.astype(F32)
    mid = rest.astype(BF16)
    low = (rest - mid.astype(F32)).astype(BF16)
    return high, mid, low


def fold_lags(spread_ref, counts):
    total = spread_ref[BAND - 1]
    for lag in range(BAND - 2, -1, -1):
        total = pltpu.roll(total, 1, 1) + spread_ref[lag]
    return rotate_each(lane_tiles(total), counts, False)


def sum_rows(totals):
    row = lax.broadcasted_iota(jnp.int32, (8, LANES), 0)
    low = row < 4
    fours = [
        jnp.where(low, totals[k], totals[k + 4]) + pltpu.roll(jnp.where(low, totals[k + 4], totals[k]), 4, 0)
        for k in range(4)
    ]

    def halve(parts, width):
        first = row & width == 0
        count = len(parts) // 2
        return [
            jnp.where(
                first,
                parts[k] + pltpu.roll(parts[k], 8 - width, 0),
                parts[k + count] + pltpu.roll(parts[k + count], width, 0),
            )
            for k in range(count)
        ]

    return halve(halve(fours, 2), 1)[0]


def quarter(tile):
    return tile[0:8] + tile[8:16] + tile[16:24] + tile[24:32]


def lanes_of(fold, tile):
    if isinstance(tile, int):
        return slice(fold * VOXELS + tile * LANES, fold * VOXELS + (tile + 1) * LANES)
    return pl.ds(pl.multiple_of(fold * VOXELS + tile * LANES, LANES), LANES)


def pick_pairs(rows_ref, column_ref, out_ref, first):
    rows = [rows_ref[block * TILES : (block + 1) * TILES, :] for block in range(BLK)]
    for place in range(N_Z):
        column = column_ref[place]
        one, two = rows[0], rows[1]
        for block in range(1, BLK - 1):
            chosen = column == block
            one = jnp.where(chosen, rows[block], one)
            two = jnp.where(chosen, rows[block + 1], two)
        out_ref[place, first : first + TILES, :] = one
        out_ref[place, first + TILES : first + 2 * TILES, :] = two


def own_kernel(core_ref, foot_ref, own_ref, half_ref, column_ref, rows_ref):
    core = core_ref[0]
    for z in range(N_Z):
        place = STEP_OUT * (z - FIRST_OUT) % N_Z
        first = foot_ref[2 * z + core] & (BLK - 1)
        column_ref[place] = jnp.broadcast_to(first[:, 0:1], (TILES, LANES))
    for tile in range(TILES):
        rows_ref[pl.ds(tile, BLK, stride=TILES), :] = own_ref[:, tile * LANES : (tile + 1) * LANES]
    pick_pairs(rows_ref, column_ref, half_ref, 0)


def other_kernel(half_ref, column_ref, other_ref, sent_ref, rows_ref):
    for tile in range(TILES):
        rows_ref[pl.ds(tile, BLK, stride=TILES), :] = other_ref[:, tile * LANES : (tile + 1) * LANES]
    for place in range(N_Z):
        sent_ref[place, 0 : 2 * TILES, :] = half_ref[place]
    pick_pairs(rows_ref, column_ref, sent_ref, 2 * TILES)


def sums_kernel(weights_ref, counts_ref, column_ref, turned_ref, row_ref, spread_ref):
    def tile_step(tile, carry):
        spread = [jnp.zeros((FOOT, LANES), F32) for _ in range(BAND)]
        rows = []
        for fold in range(FOLDS):
            total = jnp.zeros((FOOT, LANES), F32)
            for lag in range(BAND):
                weights = weights_ref[lag, :, lanes_of(fold, tile)].astype(F32)
                spread[lag] = spread[lag] + weights
                total = total + weights
            rows.append(quarter(total))
        row_ref[:, lanes_of(0, tile)] = sum_rows(rows)
        for lag in range(BAND):
            spread_ref[lag, :, lanes_of(0, tile)] = spread[lag]
        return carry

    lax.fori_loop(0, TILES, tile_step, 0)
    for tile, columns in enumerate(fold_lags(spread_ref, counts_ref[...])):
        column_ref[:, tile * LANES : (tile + 1) * LANES] = columns
        turned_ref[:, tile * LANES : (tile + 1) * LANES] = pltpu.roll(columns, SUB, 1)


def message(out_ref, peer, rows, base):
    for piece in range(PIECES):
        out_ref[peer, piece] = rows[piece * PIECE : (piece + 1) * PIECE]
    out_ref[peer, PIECES] = base


def rays_kernel(
    place_ref,
    blocks_ref,
    weights_ref,
    counts_ref,
    measured_ref,
    row_ref,
    column_ref,
    turned_ref,
    out_ref,
    window_ref,
    spread_ref,
    share_ref,
):
    core, first_block = place_ref[0], place_ref[1]
    first_owner = first_block >> 3
    odd = first_owner & 1
    double = 2 * ((lax.broadcasted_iota(jnp.int32, (8, LANES), 0) * STEP_OUT + FIRST_OUT) & (N_Z - 1))
    covered = [[] for _ in range(TILES)]
    for step in range(2):
        parity = step ^ odd
        side = parity ^ core
        owner = double + parity - first_owner
        near = (owner >= 0) & (owner < N_Z)
        turn = (FIRST_OUT - ((first_owner + 1 - parity) >> 1)) & 7
        for column in range(2):
            for tile in range(TILES):
                rows = blocks_ref[pl.ds((side * 2 + column) * TILES + tile, N_Z, stride=4 * TILES), :]
                covered[tile].append(pltpu.roll(jnp.where(near, rows[0:8], rows[8:16]), turn, 0))
    counts = counts_ref[...]
    window = jnp.concatenate(rotate_each([jnp.concatenate(c, axis=0) for c in covered], counts, True), axis=1)
    window_ref[0] = window
    for lag in range(1, BAND):
        window_ref[lag] = pltpu.roll(window, VOXELS - lag, 1)

    for tile in range(TILES):
        lanes = lanes_of(0, tile)
        windows = [window_ref[lag, :, lanes] for lag in range(BAND)]
        rows = []
        for fold in range(FOLDS):
            total = weights_ref[0, :, lanes_of(fold, tile)].astype(F32) * windows[0]
            for lag in range(1, BAND):
                total = total + weights_ref[lag, :, lanes_of(fold, tile)].astype(F32) * windows[lag]
            rows.append(quarter(total))
        share_ref[:, lanes] = (measured_ref[:, lanes] - sum_rows(rows)) / row_ref[:, lanes]
    for tile in range(TILES):
        lanes = lanes_of(0, tile)
        for lag in range(BAND):
            spread = weights_ref[lag, :, lanes].astype(F32) * share_ref[0:1, lanes]
            for fold in range(1, FOLDS):
                spread = spread + weights_ref[lag, :, lanes_of(fold, tile)].astype(F32) * share_ref[fold : fold + 1, lanes]
            spread_ref[lag, :, lanes] = spread
    low = lax.broadcasted_iota(jnp.int32, (HALF, LANES), 1) < SUB
    back = fold_lags(spread_ref, counts)
    for step in range(2):
        parity = step ^ odd
        even = [2 * (2 * tile ^ FIRST_VIEW) + parity for tile in range(TILES)]
        other = [2 * (2 * tile + 1 ^ FIRST_VIEW) + parity for tile in range(TILES)]
        base = (((first_owner + 1 - parity) >> 1) << 3) + (first_block & 7)
        base = jnp.full((PIECE, LANES), base, jnp.int32).astype(F32)
        part = slice(step * HALF, (step + 1) * HALF)
        for tile in range(TILES):
            lanes = slice(tile * LANES, (tile + 1) * LANES)
            sums = back[tile][part]
            message(out_ref, even[tile], jnp.where(low, sums, turned_ref[part, lanes]), base)
            message(out_ref, other[tile], jnp.where(low, pltpu.roll(sums, SUB, 1), column_ref[part, lanes]), base)


def place_kernel(parts_ref, out_ref):
    lane = lax.broadcasted_iota(jnp.int32, (1, LANES), 1)
    within = ((lane & 7) * BLK + ((lane >> 3) & 1)).astype(F32)
    source = lane >> 4
    targets = []
    for group in range(0, PEERS, 8):
        first = parts_ref[group, PIECES, 0:1, :]
        for other in range(1, 8):
            first = jnp.where(source == other, parts_ref[group + other, PIECES, 0:1, :], first)
        targets.append(first + within)
    target = jnp.concatenate(targets, axis=1)
    block = lax.broadcasted_iota(jnp.int32, (N_Z * BLK, PEERS * HALF), 0)
    chip = ((block >> 3) * STEP_BACK + FIRST_BACK) & (N_Z - 1)
    block = (chip * BLK + (block & (BLK - 1))).astype(F32)
    chosen = jnp.where(block == target, 1.0, 0.0).astype(BF16)
    parts = jnp.concatenate([parts_ref[peer, piece] for peer in range(PEERS) for piece in range(PIECES)], axis=0)
    high, mid, low = split3(parts)
    both = jnp.dot(chosen, jnp.concatenate([high, mid], axis=1), preferred_element_type=F32)
    total = both[:, :LANES] + (both[:, LANES:] + jnp.dot(chosen, low, preferred_element_type=F32))
    out_ref[...] = total


def finish_kernel(parts_ref, out_ref):
    total = parts_ref[0]
    for z in range(1, N_Z):
        total = total + parts_ref[z]
    columns = pltpu.roll(total, SUB, 1)
    out_ref[...] = (total / jnp.maximum(columns, 1.0))[:, :SUB]


def call(kernel, out_shape, in_specs, scratch=(), cost=None):
    return pl.pallas_call(
        kernel,
        out_shape=out_shape,
        in_specs=in_specs,
        out_specs=jax.tree.map(lambda _: VMEM, out_shape),
        scratch_shapes=scratch,
        cost_estimate=cost,
        compiler_params=pltpu.CompilerParams(vmem_limit_bytes=16 * 2**20),
    )


def shards(volume, footprint, offsets, ray_weights, measured):
    member = lax.axis_index("vol")
    core = member & 1
    swap = [(i, i ^ 1) for i in range(2 * N_Z)]
    out_chips, back_chips = (
        [[2 * ((step * place + first) % N_Z) + c for place in range(N_Z)] for c in range(2)]
        for first, step in ((FIRST_OUT, STEP_OUT), (FIRST_BACK, STEP_BACK))
    )
    planes = [
        [(2 * z + peer % 2) * N_VIEW + (peer // 2 ^ FIRST_VIEW) for peer in range(PEERS)] for z in range(N_Z)
    ]

    other = lax.ppermute(volume, "vol", swap)
    rows_scratch = pltpu.VMEM((BLK * TILES, LANES), F32)
    half, chosen = call(
        own_kernel,
        (
            jax.ShapeDtypeStruct((N_Z, 2 * TILES, LANES), F32),
            jax.ShapeDtypeStruct((N_Z, TILES, LANES), jnp.int32),
        ),
        [SMEM, VMEM, VMEM],
        [rows_scratch],
    )(core[None], footprint, volume)
    sent = call(
        other_kernel,
        jax.ShapeDtypeStruct((N_Z, 4 * TILES, LANES), F32),
        [VMEM] * 3,
        [rows_scratch],
    )(half, chosen, other)
    blocks = lax.all_to_all(sent, "vol", 0, 0, axis_index_groups=out_chips)

    weights = ray_weights.reshape(8, 2, 2, BAND, FOLDS * VOXELS)
    weights = jnp.transpose(weights, (3, 1, 2, 0, 4)).reshape(BAND, FOOT, FOLDS * VOXELS)
    counts = jnp.transpose(offsets.reshape(8, 2, 2), (1, 2, 0)).reshape(FOOT, 1)
    counts = jnp.broadcast_to(counts, (FOOT, LANES))
    work = BAND * FOOT * FOLDS * VOXELS
    columns, turned, row_sum = call(
        sums_kernel,
        (
            jax.ShapeDtypeStruct((FOOT, VOXELS), F32),
            jax.ShapeDtypeStruct((FOOT, VOXELS), F32),
            jax.ShapeDtypeStruct((FOLDS, VOXELS), F32),
        ),
        [VMEM, VMEM],
        [pltpu.VMEM((BAND, FOOT, VOXELS), F32)],
        pl.CostEstimate(flops=2 * work, bytes_accessed=2 * work, transcendentals=0),
    )(weights, counts)

    first_block = lax.dynamic_index_in_dim(footprint[:, 0, 0], member, 0, keepdims=False)
    parts = call(
        rays_kernel,
        jax.ShapeDtypeStruct((PEERS, PIECES + 1, PIECE, LANES), F32),
        [SMEM] + [VMEM] * 7,
        [
            pltpu.VMEM((BAND, FOOT, VOXELS), F32),
            pltpu.VMEM((BAND, FOOT, VOXELS), F32),
            pltpu.VMEM((FOLDS, VOXELS), F32),
        ],
        pl.CostEstimate(flops=4 * work, bytes_accessed=2 * work, transcendentals=0),
    )(
        jnp.stack([core, first_block]),
        blocks.reshape(N_Z * 4 * TILES, LANES),
        weights,
        counts,
        measured.reshape(FOLDS, VOXELS),
        row_sum,
        columns,
        turned,
    )
    parts = lax.all_to_all(parts, ("vol", "view"), 0, 0, axis_index_groups=planes)
    placed = call(place_kernel, jax.ShapeDtypeStruct((N_Z * BLK, LANES), F32), [VMEM])(parts)
    placed = lax.all_to_all(placed.reshape(N_Z, BLK, LANES), "vol", 0, 0, axis_index_groups=back_chips)
    return call(finish_kernel, jax.ShapeDtypeStruct((BLK, SUB), F32), [VMEM])(placed)


def solution(mesh):
    in_specs = (
        P("vol", None),
        P(None, "view", None),
        P("vol", "view", None),
        P("vol", "view", None, None, None),
        P("vol", "view", None),
    )
    return jax.shard_map(shards, mesh=mesh, in_specs=in_specs, out_specs=P("vol", "view"), check_vma=False)
```

```python
import jax
import jax.numpy as jnp
from jax import lax
from jax.experimental import pallas as pl
from jax.experimental.pallas import tpu as pltpu
from jax.sharding import PartitionSpec as P

VOXELS = 1024
LANES = 128
TILES = VOXELS // LANES
FOOT = 32
HALF = FOOT // 2
BAND = 4
FOLDS = 8
BLK = 8
N_Z = 16
N_VIEW = 16
PEERS = 2 * N_VIEW
PIECE = 2
PIECES = HALF // PIECE
SUB = VOXELS // N_VIEW
FIRST_OUT = 11
FIRST_BACK = 9
FIRST_VIEW = 15
STEP_OUT = 9
STEP_BACK = 1

VMEM = pl.BlockSpec(memory_space=pltpu.VMEM)
SMEM = pl.BlockSpec(memory_space=pltpu.SMEM)
F32 = jnp.float32
BF16 = jnp.bfloat16


def lane_tiles(rows):
    return [rows[:, tile * LANES : (tile + 1) * LANES] for tile in range(TILES)]


def rotate_each(tiles, counts, left):
    lane = lax.broadcasted_iota(jnp.int32, (FOOT, LANES), 1)
    within = counts & (LANES - 1)
    source = (lane + within if left else lane - within) & (LANES - 1)
    same = lane + within < LANES if left else lane >= within
    step = 1 if left else TILES - 1
    moved = [jnp.take_along_axis(tile, source, axis=1) for tile in tiles]
    tiles = [jnp.where(same, moved[t], moved[(t + step) % TILES]) for t in range(TILES)]
    for bit in range(3):
        far = step << bit
        chosen = (counts >> (7 + bit)) & 1 == 1
        tiles = [jnp.where(chosen, tiles[(t + far) % TILES], tiles[t]) for t in range(TILES)]
    return tiles


def split3(x):
    high = x.astype(BF16)
    rest = x - high.astype(F32)
    mid = rest.astype(BF16)
    low = (rest - mid.astype(F32)).astype(BF16)
    return high, mid, low


def fold_lags(spread_ref, counts):
    total = spread_ref[BAND - 1]
    for lag in range(BAND - 2, -1, -1):
        total = pltpu.roll(total, 1, 1) + spread_ref[lag]
    return rotate_each(lane_tiles(total), counts, False)


def sum_rows(totals):
    row = lax.broadcasted_iota(jnp.int32, (8, LANES), 0)
    low = row < 4
    fours = [
        jnp.where(low, totals[k], totals[k + 4]) + pltpu.roll(jnp.where(low, totals[k + 4], totals[k]), 4, 0)
        for k in range(4)
    ]

    def halve(parts, width):
        first = row & width == 0
        count = len(parts) // 2
        return [
            jnp.where(
                first,
                parts[k] + pltpu.roll(parts[k], 8 - width, 0),
                parts[k + count] + pltpu.roll(parts[k + count], width, 0),
            )
            for k in range(count)
        ]

    return halve(halve(fours, 2), 1)[0]


def quarter(tile):
    return tile[0:8] + tile[8:16] + tile[16:24] + tile[24:32]


def lanes_of(fold, tile):
    if isinstance(tile, int):
        return slice(fold * VOXELS + tile * LANES, fold * VOXELS + (tile + 1) * LANES)
    return pl.ds(pl.multiple_of(fold * VOXELS + tile * LANES, LANES), LANES)


def pick_pairs(rows_ref, column_ref, out_ref, first):
    rows = [rows_ref[block * TILES : (block + 1) * TILES, :] for block in range(BLK)]
    for place in range(N_Z):
        column = column_ref[place]
        one, two = rows[0], rows[1]
        for block in range(1, BLK - 1):
            chosen = column == block
            one = jnp.where(chosen, rows[block], one)
            two = jnp.where(chosen, rows[block + 1], two)
        out_ref[place, first : first + TILES, :] = one
        out_ref[place, first + TILES : first + 2 * TILES, :] = two


def own_kernel(core_ref, foot_ref, own_ref, half_ref, column_ref, rows_ref):
    core = core_ref[0]
    for z in range(N_Z):
        place = STEP_OUT * (z - FIRST_OUT) % N_Z
        first = foot_ref[2 * z + core] & (BLK - 1)
        column_ref[place] = jnp.broadcast_to(first[:, 0:1], (TILES, LANES))
    for tile in range(TILES):
        rows_ref[pl.ds(tile, BLK, stride=TILES), :] = own_ref[:, tile * LANES : (tile + 1) * LANES]
    pick_pairs(rows_ref, column_ref, half_ref, 0)


def other_kernel(half_ref, column_ref, other_ref, sent_ref, rows_ref):
    for tile in range(TILES):
        rows_ref[pl.ds(tile, BLK, stride=TILES), :] = other_ref[:, tile * LANES : (tile + 1) * LANES]
    for place in range(N_Z):
        sent_ref[place, 0 : 2 * TILES, :] = half_ref[place]
    pick_pairs(rows_ref, column_ref, sent_ref, 2 * TILES)


def sums_kernel(weights_ref, counts_ref, column_ref, turned_ref, row_ref, spread_ref):
    def tile_step(tile, carry):
        spread = [jnp.zeros((FOOT, LANES), F32) for _ in range(BAND)]
        rows = []
        for fold in range(FOLDS):
            total = jnp.zeros((FOOT, LANES), F32)
            for lag in range(BAND):
                weights = weights_ref[lag, :, lanes_of(fold, tile)].astype(F32)
                spread[lag] = spread[lag] + weights
                total = total + weights
            rows.append(quarter(total))
        row_ref[:, lanes_of(0, tile)] = sum_rows(rows)
        for lag in range(BAND):
            spread_ref[lag, :, lanes_of(0, tile)] = spread[lag]
        return carry

    lax.fori_loop(0, TILES, tile_step, 0)
    for tile, columns in enumerate(fold_lags(spread_ref, counts_ref[...])):
        column_ref[:, tile * LANES : (tile + 1) * LANES] = columns
        turned_ref[:, tile * LANES : (tile + 1) * LANES] = pltpu.roll(columns, SUB, 1)


def message(out_ref, peer, rows, base):
    for piece in range(PIECES):
        out_ref[peer, piece] = rows[piece * PIECE : (piece + 1) * PIECE]
    out_ref[peer, PIECES] = base


def rays_kernel(
    place_ref,
    blocks_ref,
    weights_ref,
    counts_ref,
    measured_ref,
    row_ref,
    column_ref,
    turned_ref,
    out_ref,
    window_ref,
    spread_ref,
    share_ref,
):
    core, first_block = place_ref[0], place_ref[1]
    first_owner = first_block >> 3
    odd = first_owner & 1
    double = 2 * ((lax.broadcasted_iota(jnp.int32, (8, LANES), 0) * STEP_OUT + FIRST_OUT) & (N_Z - 1))
    covered = [[] for _ in range(TILES)]
    for step in range(2):
        parity = step ^ odd
        side = parity ^ core
        owner = double + parity - first_owner
        near = (owner >= 0) & (owner < N_Z)
        turn = (FIRST_OUT - ((first_owner + 1 - parity) >> 1)) & 7
        for column in range(2):
            for tile in range(TILES):
                rows = blocks_ref[pl.ds((side * 2 + column) * TILES + tile, N_Z, stride=4 * TILES), :]
                covered[tile].append(pltpu.roll(jnp.where(near, rows[0:8], rows[8:16]), turn, 0))
    counts = counts_ref[...]
    window = jnp.concatenate(rotate_each([jnp.concatenate(c, axis=0) for c in covered], counts, True), axis=1)
    window_ref[0] = window
    for lag in range(1, BAND):
        window_ref[lag] = pltpu.roll(window, VOXELS - lag, 1)

    for tile in range(TILES):
        lanes = lanes_of(0, tile)
        windows = [window_ref[lag, :, lanes] for lag in range(BAND)]
        rows = []
        for fold in range(FOLDS):
            total = weights_ref[0, :, lanes_of(fold, tile)].astype(F32) * windows[0]
            for lag in range(1, BAND):
                total = total + weights_ref[lag, :, lanes_of(fold, tile)].astype(F32) * windows[lag]
            rows.append(quarter(total))
        share_ref[:, lanes] = (measured_ref[:, lanes] - sum_rows(rows)) / row_ref[:, lanes]
    for tile in range(TILES):
        lanes = lanes_of(0, tile)
        for lag in range(BAND):
            spread = weights_ref[lag, :, lanes].astype(F32) * share_ref[0:1, lanes]
            for fold in range(1, FOLDS):
                spread = spread + weights_ref[lag, :, lanes_of(fold, tile)].astype(F32) * share_ref[fold : fold + 1, lanes]
            spread_ref[lag, :, lanes] = spread
    low = lax.broadcasted_iota(jnp.int32, (HALF, LANES), 1) < SUB
    back = fold_lags(spread_ref, counts)
    for step in range(2):
        parity = step ^ odd
        first = parity * N_VIEW
        even = [first + (2 * tile ^ FIRST_VIEW) for tile in range(TILES)]
        other = [first + (2 * tile + 1 ^ FIRST_VIEW) for tile in range(TILES)]
        base = (((first_owner + 1 - parity) >> 1) << 3) + (first_block & 7)
        base = jnp.full((PIECE, LANES), base, jnp.int32).astype(F32)
        part = slice(step * HALF, (step + 1) * HALF)
        for tile in range(TILES):
            lanes = slice(tile * LANES, (tile + 1) * LANES)
            sums = back[tile][part]
            message(out_ref, even[tile], jnp.where(low, sums, turned_ref[part, lanes]), base)
            message(out_ref, other[tile], jnp.where(low, pltpu.roll(sums, SUB, 1), column_ref[part, lanes]), base)


def place_kernel(parts_ref, out_ref):
    lane = lax.broadcasted_iota(jnp.int32, (1, LANES), 1)
    within = ((lane & 7) * BLK + ((lane >> 3) & 1)).astype(F32)
    source = lane >> 4
    targets = []
    for group in range(0, PEERS, 8):
        first = parts_ref[group, PIECES, 0:1, :]
        for other in range(1, 8):
            first = jnp.where(source == other, parts_ref[group + other, PIECES, 0:1, :], first)
        targets.append(first + within)
    target = jnp.concatenate(targets, axis=1)
    block = lax.broadcasted_iota(jnp.int32, (N_Z * BLK, PEERS * HALF), 0)
    chip = ((block >> 3) * STEP_BACK + FIRST_BACK) & (N_Z - 1)
    block = (chip * BLK + (block & (BLK - 1))).astype(F32)
    chosen = jnp.where(block == target, 1.0, 0.0).astype(BF16)
    parts = jnp.concatenate([parts_ref[peer, piece] for peer in range(PEERS) for piece in range(PIECES)], axis=0)
    high, mid, low = split3(parts)
    both = jnp.dot(chosen, jnp.concatenate([high, mid], axis=1), preferred_element_type=F32)
    total = both[:, :LANES] + (both[:, LANES:] + jnp.dot(chosen, low, preferred_element_type=F32))
    out_ref[...] = total


def finish_kernel(parts_ref, out_ref):
    total = parts_ref[0]
    for z in range(1, N_Z):
        total = total + parts_ref[z]
    columns = pltpu.roll(total, SUB, 1)
    out_ref[...] = (total / jnp.maximum(columns, 1.0))[:, :SUB]


def call(kernel, out_shape, in_specs, scratch=(), cost=None):
    return pl.pallas_call(
        kernel,
        out_shape=out_shape,
        in_specs=in_specs,
        out_specs=jax.tree.map(lambda _: VMEM, out_shape),
        scratch_shapes=scratch,
        cost_estimate=cost,
        compiler_params=pltpu.CompilerParams(vmem_limit_bytes=16 * 2**20),
    )


def shards(volume, footprint, offsets, ray_weights, measured):
    member = lax.axis_index("vol")
    core = member & 1
    swap = [(i, i ^ 1) for i in range(2 * N_Z)]
    out_chips, back_chips = (
        [[2 * ((step * place + first) % N_Z) + c for place in range(N_Z)] for c in range(2)]
        for first, step in ((FIRST_OUT, STEP_OUT), (FIRST_BACK, STEP_BACK))
    )
    planes = [[z * PEERS + (peer ^ FIRST_VIEW) for peer in range(PEERS)] for z in range(N_Z)]

    other = lax.ppermute(volume, "vol", swap)
    rows_scratch = pltpu.VMEM((BLK * TILES, LANES), F32)
    half, chosen = call(
        own_kernel,
        (
            jax.ShapeDtypeStruct((N_Z, 2 * TILES, LANES), F32),
            jax.ShapeDtypeStruct((N_Z, TILES, LANES), jnp.int32),
        ),
        [SMEM, VMEM, VMEM],
        [rows_scratch],
    )(core[None], footprint, volume)
    sent = call(
        other_kernel,
        jax.ShapeDtypeStruct((N_Z, 4 * TILES, LANES), F32),
        [VMEM] * 3,
        [rows_scratch],
    )(half, chosen, other)
    blocks = lax.all_to_all(sent, "vol", 0, 0, axis_index_groups=out_chips)

    weights = ray_weights.reshape(8, 2, 2, BAND, FOLDS * VOXELS)
    weights = jnp.transpose(weights, (3, 1, 2, 0, 4)).reshape(BAND, FOOT, FOLDS * VOXELS)
    counts = jnp.transpose(offsets.reshape(8, 2, 2), (1, 2, 0)).reshape(FOOT, 1)
    counts = jnp.broadcast_to(counts, (FOOT, LANES))
    work = BAND * FOOT * FOLDS * VOXELS
    columns, turned, row_sum = call(
        sums_kernel,
        (
            jax.ShapeDtypeStruct((FOOT, VOXELS), F32),
            jax.ShapeDtypeStruct((FOOT, VOXELS), F32),
            jax.ShapeDtypeStruct((FOLDS, VOXELS), F32),
        ),
        [VMEM, VMEM],
        [pltpu.VMEM((BAND, FOOT, VOXELS), F32)],
        pl.CostEstimate(flops=2 * work, bytes_accessed=2 * work, transcendentals=0),
    )(weights, counts)

    first_block = lax.dynamic_index_in_dim(footprint[:, 0, 0], member, 0, keepdims=False)
    parts = call(
        rays_kernel,
        jax.ShapeDtypeStruct((PEERS, PIECES + 1, PIECE, LANES), F32),
        [SMEM] + [VMEM] * 7,
        [
            pltpu.VMEM((BAND, FOOT, VOXELS), F32),
            pltpu.VMEM((BAND, FOOT, VOXELS), F32),
            pltpu.VMEM((FOLDS, VOXELS), F32),
        ],
        pl.CostEstimate(flops=4 * work, bytes_accessed=2 * work, transcendentals=0),
    )(
        jnp.stack([core, first_block]),
        blocks.reshape(N_Z * 4 * TILES, LANES),
        weights,
        counts,
        measured.reshape(FOLDS, VOXELS),
        row_sum,
        columns,
        turned,
    )
    parts = lax.all_to_all(parts, ("vol", "view"), 0, 0, axis_index_groups=planes)
    placed = call(place_kernel, jax.ShapeDtypeStruct((N_Z * BLK, LANES), F32), [VMEM])(parts)
    placed = lax.all_to_all(placed.reshape(N_Z, BLK, LANES), "vol", 0, 0, axis_index_groups=back_chips)
    return call(finish_kernel, jax.ShapeDtypeStruct((BLK, SUB), F32), [VMEM])(placed)


def solution(mesh):
    in_specs = (
        P("vol", None),
        P(None, "view", None),
        P("vol", "view", None),
        P("vol", "view", None, None, None),
        P("vol", "view", None),
    )
    return jax.shard_map(shards, mesh=mesh, in_specs=in_specs, out_specs=P("vol", "view"), check_vma=False)
```
